256 devices in a mesh: dp: 16 (over x, y_hi, core), fsdp: 16 (over z, y_lo).
Axes of the slice: x: 4, y: 4 (y_hi: 2, y_lo: 2; y = y_hi * 2 + y_lo), z: 8, core: 2. Of those that a mesh axis runs over, the one named last changes fastest.
Arguments:
- patches: bfloat16 [16, 224, 8, 8, 768], P('fsdp', 'dp'), may hold values from -6 to 6
- out_grad: bfloat16 [16, 224, 8, 8, 768], P('fsdp', 'dp'), may hold values from -6 to 6
- row_counts: int32 [16, 16], P('fsdp', 'dp'), may hold values from 2 to 14, as said below
- dw_kernel: bfloat16 [49, 768], P(None, 'fsdp'), may hold values from -0.875 to 0.875
- ln_gain: bfloat16 [768], P('fsdp'), may hold values from 0.099609375 to 1.8984375
- ln_bias: bfloat16 [768], P('fsdp'), may hold values from -3 to 3
- w_first: bfloat16 [768, 2304], P('fsdp'), may hold values from -0.21875 to 0.21875
- first_bias: bfloat16 [2304], P('fsdp'), may hold values from -3 to 3
- w_second: bfloat16 [2304, 768], P('fsdp'), may hold values from -0.125 to 0.125
- layer_scale: bfloat16 [768], P('fsdp'), may hold values from 0.25 to 1
Outputs:
- in_grad: float32 [16, 224, 8, 8, 768], P('fsdp', 'dp')
- grad_first: float32 [768, 2304], P('fsdp')
- grad_second: float32 [2304, 768], P('fsdp')
- grad_kernel: float32 [49, 768], P(None, 'fsdp')
- grad_bias: float32 [2304], P('fsdp')
- grad_channels: float32 [3, 768], P(None, 'fsdp')
The draws below stay inside these ranges and needn't reach their ends.
Inputs may be any that keep to these rules, and one draw needn't show every extreme that they name: In every column f the 16 counts row_counts[f, :] sum to exactly 128, and some device of every column holds 14 live slots.
All inputs are finite; a program needn't handle non-finite values.
Results may differ from the reference program's by a relative error of at most 0.007.
Values may be sent and summed in bfloat16 or wider, within the bound.
No kernel may reach another device: no remote copies, remote signals or barrier semaphores. Data moves between devices by JAX's collectives and lax.ppermute only.
A program may use at most 192 MiB of HBM per device.

```python
import math
import jax
import jax.numpy as jnp
from jax import lax

C = 768
FF = 2304
SIDE = 8
ROWS = 8
OWN = 14
TOKENS = 131072
N_DP = 16
N_FSDP = 16


def draw_row_counts(key, part):
    column_keys = jax.random.split(key, N_FSDP)

    def column(column_key):
        first_key, second_key = jax.random.split(column_key)
        upper = jax.random.randint(first_key, (N_DP // 2,), 2, OWN + 1)
        upper = upper.at[0].set(OWN)
        lower = 2 * ROWS - upper
        values = jnp.stack([upper, lower], axis=1).reshape(-1)
        order = jax.random.permutation(second_key, N_DP)
        return values[jnp.argsort(order)]
    return jax.vmap(column)(column_keys).astype(jnp.int32)


def block_scale(rng, shape, cuts, smallest, high):
    def one(dim, shards_of):
        draws = jax.random.uniform(jax.random.fold_in(jax.random.fold_in(rng, 6), dim), (shards_of,), jnp.float32, smallest / len(cuts), high / len(cuts))
        return jnp.repeat(jnp.exp(draws), shape[dim] // shards_of).reshape((-1,) + (1,) * (len(shape) - dim - 1))

    factor_of = one(*cuts[0])
    for cut in cuts[1:]:
        factor_of = factor_of * one(*cut)
    return factor_of


def scatter_about(own_key, dims, deviation, reach, shards=(), kind=jnp.bfloat16):
    values = deviation * jax.random.normal(own_key, dims, jnp.float32)
    if shards:
        values = values * block_scale(own_key, dims, shards, -0.22, 0.18)
    return jnp.clip(values, -reach, reach).astype(kind)


def setup_inputs(seed: int = 0) -> dict:
    streams_of = jax.random.split(jax.random.key(seed), 11)
    return {
        "patches": scatter_about(streams_of[0], (N_FSDP, N_DP * OWN, SIDE, SIDE, C), 1.0, 6.0, ((0, 16), (1, 16))),
        "out_grad": scatter_about(streams_of[1], (N_FSDP, N_DP * OWN, SIDE, SIDE, C), 1.0, 6.0, ((0, 16), (1, 16))),
        "row_counts": draw_row_counts(jax.random.fold_in(streams_of[10], 71), 0),
        "dw_kernel": scatter_about(streams_of[3], (49, C), 49 ** -0.5, 0.875, ((1, 16),)),
        "ln_gain": jnp.clip(1.0 + 0.18 * jax.random.normal(streams_of[4], (C,), jnp.float32), 0.099609375, 1.8984375).astype(jnp.bfloat16),
        "ln_bias": scatter_about(streams_of[5], (C,), 0.5, 3.0, ((0, 16),)),
        "w_first": scatter_about(streams_of[6], (C, FF), C ** -0.5, 0.21875, ((0, 16),)),
        "first_bias": scatter_about(streams_of[7], (FF,), 0.5, 3.0, ((0, 16),)),
        "w_second": scatter_about(streams_of[8], (FF, C), FF ** -0.5, 0.125, ((0, 16),)),
        "layer_scale": jnp.clip(jnp.exp(math.log(1.0) - 1.3862944 * jax.random.uniform(streams_of[9], (C,), jnp.float32) ** block_scale(streams_of[9], (C,), ((0, 16),), -0.2, 0.2)), 0.25, 1.0).astype(jnp.bfloat16),
    }


def block_pass(patch_in, cotangent, weights):
    kernel, gain, shift, first, first_bias, second, layer_scale = weights
    patch_count, extent, _, channels = patch_in.shape
    padded = jnp.pad(patch_in, ((0, 0), (3, 3), (3, 3), (0, 0)))
    kernel_f = kernel.astype(jnp.float32)
    conv = jnp.zeros((patch_count, extent, extent, channels), jnp.float32)
    for tap_row in range(7):
        for tap_col in range(7):
            window = padded[:, tap_row:tap_row + extent, tap_col:tap_col + extent, :].astype(jnp.float32)
            conv = conv + window * kernel_f[tap_row * 7 + tap_col]
    average = lax.optimization_barrier(jnp.mean(conv, axis=-1, keepdims=True))
    centred = conv - average
    variance = lax.optimization_barrier(jnp.mean(centred * centred, axis=-1, keepdims=True))
    inverse = lax.rsqrt(variance + 1e-06)
    standard = centred * inverse
    gain_f = gain.astype(jnp.float32)
    normed = (standard * gain_f + shift.astype(jnp.float32)).astype(jnp.bfloat16)
    flat_rows = normed.reshape(-1, channels)
    preact = jnp.dot(flat_rows, first, preferred_element_type=jnp.float32) + first_bias.astype(jnp.float32)
    normal_prob = 0.5 * (1.0 + jax.scipy.special.erf(preact * 0.7071067811865476))
    hidden = (preact * normal_prob).astype(jnp.bfloat16)
    branch = jnp.dot(hidden, second, preferred_element_type=jnp.float32)
    cot_float = cotangent.reshape(-1, channels).astype(jnp.float32)
    scale_term = lax.optimization_barrier(jnp.sum(cot_float * branch, axis=0))
    grad_branch = (cot_float * layer_scale.astype(jnp.float32)).astype(jnp.bfloat16)
    grad_second = jnp.dot(hidden.T, grad_branch, preferred_element_type=jnp.float32)
    grad_hidden = jnp.dot(grad_branch, second.T, preferred_element_type=jnp.float32)
    slope = normal_prob + preact * jnp.exp(-0.5 * preact * preact) * 0.3989422804014327
    grad_preact = (grad_hidden * slope).astype(jnp.bfloat16)
    grad_first = jnp.dot(flat_rows.T, grad_preact, preferred_element_type=jnp.float32)
    grad_bias = lax.optimization_barrier(jnp.sum(grad_preact.astype(jnp.float32), axis=0))
    grad_normed = jnp.dot(grad_preact, first.T, preferred_element_type=jnp.float32).reshape(patch_count, extent, extent, channels)
    gain_term = lax.optimization_barrier(jnp.sum(grad_normed * standard, axis=(0, 1, 2)))
    shift_term = lax.optimization_barrier(jnp.sum(grad_normed, axis=(0, 1, 2)))
    grad_std = grad_normed * gain_f
    grad_conv = inverse * (grad_std - lax.optimization_barrier(jnp.mean(grad_std, axis=-1, keepdims=True)) - standard * lax.optimization_barrier(jnp.mean(grad_std * standard, axis=-1, keepdims=True)))
    grad_pad = jnp.pad(grad_conv, ((0, 0), (3, 3), (3, 3), (0, 0)))
    kernel_terms = []
    grad_input = jnp.zeros((patch_count, extent, extent, channels), jnp.float32)
    for tap_row in range(7):
        for tap_col in range(7):
            window = padded[:, tap_row:tap_row + extent, tap_col:tap_col + extent, :].astype(jnp.float32)
            kernel_terms.append(lax.optimization_barrier(jnp.sum(grad_conv * window, axis=(0, 1, 2))))
            back_window = grad_pad[:, 6 - tap_row:6 - tap_row + extent, 6 - tap_col:6 - tap_col + extent, :]
            grad_input = grad_input + back_window * kernel_f[tap_row * 7 + tap_col]
    in_grad = cotangent.astype(jnp.float32) + grad_input
    channel_terms = jnp.stack([gain_term, shift_term, scale_term])
    return (in_grad, (grad_first, grad_second, jnp.stack(kernel_terms), grad_bias, channel_terms))

def live_index(column_counts):
    owners = column_counts.shape[0]
    starts = jnp.cumsum(column_counts) - column_counts
    ends = starts + column_counts
    order = jnp.arange(owners * ROWS, dtype=jnp.int32)
    owner_hit = ((order[:, None] >= starts[None, :]) & (order[:, None] < ends[None, :])).astype(jnp.int32)
    owner_ids = lax.optimization_barrier(jnp.sum(owner_hit * jnp.arange(owners, dtype=jnp.int32)[None, :], axis=1))
    row_ids = order - lax.optimization_barrier(jnp.sum(owner_hit * starts[None, :], axis=1))
    return (owner_ids * OWN + row_ids).astype(jnp.int32)

def reference(patches, out_grad, row_counts, dw_kernel, ln_gain, ln_bias, w_first, first_bias, w_second, layer_scale):
    weights = (dw_kernel, ln_gain, ln_bias, w_first, first_bias, w_second, layer_scale)

    def column(carry, items):
        column_in, column_cot, column_counts = items
        chosen = live_index(column_counts)
        live_in = jnp.take(column_in, chosen, axis=0)
        live_cot = jnp.take(column_cot, chosen, axis=0)
        live_grad, terms = block_pass(live_in, live_cot, weights)
        placed = jnp.zeros(column_in.shape, jnp.float32).at[chosen].set(live_grad)
        summed = tuple((left + right for left, right in zip(carry, terms)))
        return (summed, placed)
    channels = patches.shape[4]
    hidden_units = w_first.shape[1]
    start = (jnp.zeros((channels, hidden_units), jnp.float32), jnp.zeros((hidden_units, channels), jnp.float32), jnp.zeros((49, channels), jnp.float32), jnp.zeros((hidden_units,), jnp.float32), jnp.zeros((3, channels), jnp.float32))
    totals, in_grad = lax.scan(column, start, (patches, out_grad, row_counts))
    factor = 1.0 / math.sqrt(TOKENS)
    return (in_grad, totals[0] * factor, totals[1] * factor, totals[2] * factor, totals[3] * factor, totals[4] * factor)
```

```python
import functools
import math

import jax
import jax.numpy as jnp
from jax import lax
from jax.experimental import pallas as pl
from jax.experimental.pallas import tpu as pltpu
from jax.sharding import PartitionSpec as P

ROWS = 8
LANES = 128
SUBLANES = 8
SIDE = 8
SPOTS = SIDE * SIDE
REACH = 3
TAPS = 7
BLOCK = 256
TOKEN_BLOCK = 448
CUT = 384
AXES = ("dp", "fsdp")
X, Y, Z = 4, 4, 8
BF16, F32 = jnp.bfloat16, jnp.float32
VMEM_LIMIT = 56 * 1024 * 1024


def whole(shape):
    return pl.BlockSpec(shape, lambda *_: (0,) * len(shape))


def spread_taps(taps_ref, spread):
    for tap in range(TAPS * TAPS):
        spread[tap] = jnp.broadcast_to(taps_ref[tap : tap + 1, :], (SUBLANES, LANES))


def to_patch_minor(rows, out, groups):
    def one(spot, _):
        for group in range(groups):
            out[group * SPOTS + spot] = rows[
                pl.ds(group * SUBLANES * SPOTS + spot, SUBLANES, stride=SPOTS), :
            ]
        return 0

    lax.fori_loop(0, SPOTS, one, 0, unroll=8)


def conv_rows(src, spread, group, flip, emit):
    for p in range(SIDE):
        sums = [None] * SIDE
        for a in range(TAPS):
            row = p + a - REACH
            if not 0 <= row < SIDE:
                continue
            values = [src[group * SPOTS + row * SIDE + q] for q in range(SIDE)]
            for b in range(TAPS):
                tap = a * TAPS + b
                weight = spread[TAPS * TAPS - 1 - tap if flip else tap]
                for q in range(SIDE):
                    col = q + b - REACH
                    if 0 <= col < SIDE:
                        term = values[col] * weight
                        sums[q] = term if sums[q] is None else sums[q] + term
        for q in range(SIDE):
            emit(p * SIDE + q, sums[q])


def forward_kernel(
    slots, x_ref, g_ref, count_ref, taps_ref, gain_ref, shift_ref, scale_ref,
    normed_ref, std_ref, inv_ref, gb_ref,
    rows, minor, spread, conv,
):
    step = pl.program_id(0)
    groups = rows.shape[0] // (SUBLANES * SPOTS)
    channels = conv.shape[0] * LANES
    spread_taps(taps_ref, spread)

    def load(slot, _):
        rows[pl.ds(pl.multiple_of(slot * SPOTS, SPOTS), SPOTS), :] = (
            x_ref[slot].astype(F32).reshape(SPOTS, LANES)
        )
        return 0

    lax.fori_loop(0, slots, load, 0)
    to_patch_minor(rows, minor, groups)

    def convolve(group, _):
        def emit(spot, value):
            conv[step, pl.ds(group * SUBLANES * SPOTS + spot, SUBLANES, stride=SPOTS), :] = value

        conv_rows(minor, spread, group, False, emit)
        return 0

    lax.fori_loop(0, groups, convolve, 0)

    @pl.when(step == conv.shape[0] - 1)
    def _():
        count = count_ref[0, 0]
        gain = [gain_ref[:, c * LANES : (c + 1) * LANES] for c in range(conv.shape[0])]
        shift = [shift_ref[:, c * LANES : (c + 1) * LANES] for c in range(conv.shape[0])]
        scale = [scale_ref[:, c * LANES : (c + 1) * LANES] for c in range(conv.shape[0])]
        tall = 32

        def norm(i, _):
            at = pl.ds(pl.multiple_of(i * tall, tall), tall)
            parts = [conv[c, at, :] for c in range(conv.shape[0])]
            mean = sum(jnp.sum(v, axis=1, keepdims=True) for v in parts) / channels
            parts = [v - mean for v in parts]
            var = sum(jnp.sum(v * v, axis=1, keepdims=True) for v in parts) / channels
            inv = lax.rsqrt(var + 1e-06)
            inv_ref[at, :] = inv
            for c, v in enumerate(parts):
                lanes = slice(c * LANES, (c + 1) * LANES)
                std = v * inv
                std_ref[at, lanes] = std
                normed_ref[at, lanes] = (std * gain[c] + shift[c]).astype(BF16)
            return 0

        lax.fori_loop(0, slots * SPOTS // tall, norm, 0)

        def cotangent(slot, _):
            at = pl.ds(pl.multiple_of(slot * SPOTS, SPOTS), SPOTS)
            live = jnp.where(slot < count, 1.0, 0.0)
            for c in range(conv.shape[0]):
                lanes = slice(c * LANES, (c + 1) * LANES)
                g = g_ref[slot, :, :, lanes].astype(F32).reshape(SPOTS, LANES)
                gb_ref[at, lanes] = (g * (scale[c] * live)).astype(BF16)
            return 0

        lax.fori_loop(0, slots, cotangent, 0)


def forward(x, g, count, taps, gain, shift, scale):
    slots, channels = x.shape[0], x.shape[3]
    tokens, parts = slots * SPOTS, channels // LANES
    groups = -(-slots // SUBLANES)
    padded = groups * SUBLANES * SPOTS
    return pl.pallas_call(
        functools.partial(forward_kernel, slots),
        grid=(parts,),
        in_specs=[
            pl.BlockSpec((slots, SIDE, SIDE, LANES), lambda j: (0, 0, 0, j)),
            whole((slots, SIDE, SIDE, channels)),
            pl.BlockSpec(memory_space=pltpu.SMEM),
            pl.BlockSpec((TAPS * TAPS, LANES), lambda j: (0, j)),
            whole((1, channels)),
            whole((1, channels)),
            whole((1, channels)),
        ],
        out_specs=[
            whole((tokens, channels)),
            whole((tokens, channels)),
            whole((tokens, 1)),
            whole((tokens, channels)),
        ],
        out_shape=[
            jax.ShapeDtypeStruct((tokens, channels), BF16),
            jax.ShapeDtypeStruct((tokens, channels), F32),
            jax.ShapeDtypeStruct((tokens, 1), F32),
            jax.ShapeDtypeStruct((tokens, channels), BF16),
        ],
        scratch_shapes=[
            pltpu.VMEM((padded, LANES), F32),
            pltpu.VMEM((groups * SPOTS, SUBLANES, LANES), F32),
            pltpu.VMEM((TAPS * TAPS, SUBLANES, LANES), F32),
            pltpu.VMEM((parts, padded, LANES), F32),
        ],
        compiler_params=pltpu.CompilerParams(vmem_limit_bytes=VMEM_LIMIT),
        cost_estimate=pl.CostEstimate(
            flops=2 * 49 * tokens * channels, bytes_accessed=12 * tokens * channels, transcendentals=0
        ),
        name="forward",
    )(x, g, count, taps, gain, shift, scale)


def mlp_kernel(
    shards, core_ref, order_ref, mine_ref, theirs_ref, gb_mine_ref, gb_theirs_ref, bias_ref, second_ref,
    *refs,
):
    pieces = refs[:shards]
    (
    grad_first_ref, grad_second_mine_ref, grad_second_theirs_ref, gn_mine_ref, gn_theirs_ref,
    grad_bias_ref, scale_ref,
    first, second, sum_first, sum_second, flipped, sems,
    ) = refs[shards:]
    step = pl.program_id(0)
    steps = pl.num_programs(0)
    core = core_ref[0]
    height = pieces[0].shape[0]
    channels, hidden = first.shape
    own = channels // shards
    cuts = hidden // CUT
    units = height - own * cuts
    dot = functools.partial(lax.dot_general, preferred_element_type=F32)

    def copies():
        made = []
        for i, piece in enumerate(pieces):
            f = order_ref[i]
            for k in range(cuts):
                made.append(
                    pltpu.make_async_copy(
                        piece.at[pl.ds(k * own, own), :],
                        first.at[pl.ds(pl.multiple_of(f * own, own), own), pl.ds(k * CUT, CUT)],
                        sems.at[i],
                    )
                )
            made.append(
                pltpu.make_async_copy(
                    piece.at[pl.ds(cuts * own, units), :],
                    second.at[
                        pl.ds(pl.multiple_of(lax.rem(f + core * (shards // 2), shards) * units, units), units),
                        pl.ds(pl.multiple_of(core * CUT, CUT), CUT),
                    ],
                    sems.at[i],
                )
            )
        for f in range(shards // 2):
            made.append(
                pltpu.make_async_copy(
                    second_ref.at[f],
                    second.at[
                        pl.ds(f * units, units), pl.ds(pl.multiple_of((1 - core) * CUT, CUT), CUT)
                    ],
                    sems.at[shards],
                )
            )
        return made

    @pl.when(step == 0)
    def _():
        made = copies()
        for copy in made:
            copy.start()
        for copy in made:
            copy.wait()
        scale_ref[...] = jnp.zeros_like(scale_ref)
        grad_bias_ref[...] = jnp.zeros_like(grad_bias_ref)
        sum_first[...] = jnp.zeros_like(sum_first)
        sum_second[...] = jnp.zeros_like(sum_second)

    def block(normed, gb):
        flipped[...] = normed.T
        grad_normed = None
        for start in range(0, hidden, BLOCK):
            wide = min(BLOCK, hidden - start)
            at = slice(start, start + wide)
            preact = dot(normed, first[:, at], (((1,), (0,)), ((), ()))) + bias_ref[:, at]
            grad_hidden = dot(gb, second[at, :], (((1,), (1,)), ((), ())))
            prob = 0.5 * (1.0 + lax.erf(preact * 0.7071067811865476))
            active = (preact * prob).astype(BF16)
            slope = prob + preact * jnp.exp(-0.5 * preact * preact) * 0.3989422804014327
            grad_preact = (grad_hidden * slope).astype(BF16)
            sum_second[at, :] += dot(active, gb, (((0,), (0,)), ((), ())))
            sum_first[:, at] += dot(flipped[...], grad_preact, (((1,), (0,)), ((), ())))
            grad_bias_ref[:, at] += jnp.sum(grad_preact.astype(F32), axis=0, keepdims=True)
            part = dot(grad_preact, first[:, at], (((1,), (1,)), ((), ())))
            grad_normed = part if grad_normed is None else grad_normed + part
        return grad_normed

    @pl.when(step < steps // 2)
    def _():
        gn_mine_ref[...] = block(mine_ref[...], gb_mine_ref[...])

    @pl.when(step >= steps // 2)
    def _():
        gn_theirs_ref[...] = block(theirs_ref[...], gb_theirs_ref[...]).astype(BF16)

    @pl.when(step == steps - 1)
    def _():
        scale_ref[...] = jnp.sum(
            sum_second[...] * second[:hidden, :].astype(F32), axis=0, keepdims=True
        )
        for f in range(shards):
            for k in range(cuts):
                grad_first_ref[f, k * own : (k + 1) * own, :] = sum_first[
                    f * own : (f + 1) * own, k * CUT : (k + 1) * CUT
                ].astype(BF16)
        for side in range(2):
            to = [grad_second_mine_ref, grad_second_theirs_ref]

            @pl.when(core == side)
            def _():
                for f in range(shards // 2):
                    rows = slice(f * units, (f + 1) * units)
                    for half in range(2):
                        to[half != side][f] = sum_second[
                            rows, half * CUT : (half + 1) * CUT
                        ].astype(BF16)


def mlp(core, order, mine, theirs, gb_mine, gb_theirs, bias, second, pieces):
    tokens, channels = mine.shape
    shards = len(pieces)
    hidden = bias.shape[1]
    units = second.shape[1]
    steps = tokens // TOKEN_BLOCK
    early = pl.BlockSpec((TOKEN_BLOCK, channels), lambda j: (jnp.minimum(j, steps - 1), 0))
    late = pl.BlockSpec((TOKEN_BLOCK, channels), lambda j: (jnp.maximum(j - steps, 0), 0))
    anywhere = pl.BlockSpec(memory_space=pl.ANY)
    half = (shards // 2, units, CUT)
    return pl.pallas_call(
        functools.partial(mlp_kernel, shards),
        grid=(2 * steps,),
        in_specs=[
            pl.BlockSpec(memory_space=pltpu.SMEM),
            pl.BlockSpec(memory_space=pltpu.SMEM),
            early, late, early, late,
            whole((1, hidden)),
            anywhere,
        ]
        + [anywhere] * shards,
        out_specs=[
            whole((shards, hidden // CUT * (channels // shards), CUT)),
            whole(half), whole(half),
            early, late,
            whole((1, hidden)),
            whole((1, channels)),
        ],
        out_shape=[
            jax.ShapeDtypeStruct((shards, hidden // CUT * (channels // shards), CUT), BF16),
            jax.ShapeDtypeStruct(half, BF16),
            jax.ShapeDtypeStruct(half, BF16),
            jax.ShapeDtypeStruct((tokens, channels), F32),
            jax.ShapeDtypeStruct((tokens, channels), BF16),
            jax.ShapeDtypeStruct((1, hidden), F32),
            jax.ShapeDtypeStruct((1, channels), F32),
        ],
        scratch_shapes=[
            pltpu.VMEM((channels, hidden), BF16),
            pltpu.VMEM((2 * hidden, channels), BF16),
            pltpu.VMEM((channels, hidden), F32),
            pltpu.VMEM((hidden, channels), F32),
            pltpu.VMEM((channels, TOKEN_BLOCK), BF16),
            pltpu.SemaphoreType.DMA((shards + 1,)),
        ],
        compiler_params=pltpu.CompilerParams(vmem_limit_bytes=VMEM_LIMIT),
        cost_estimate=pl.CostEstimate(
            flops=20 * tokens * channels * hidden,
            bytes_accessed=12 * hidden * channels,
            transcendentals=4 * tokens * hidden,
        ),
        name="mlp",
    )(core, order, mine, theirs, gb_mine, gb_theirs, bias, second, *pieces)


def backward_kernel(
    slots, x_ref, g_ref, count_ref, taps_ref, gain_ref, std_ref, inv_ref, gn_ref, gn_other_ref,
    in_grad_ref, grad_taps_ref, channel_ref,
    rows, minor, grad_minor, spread, grad_conv, result, tap_sums,
):
    step = pl.program_id(0)
    parts = grad_conv.shape[0]
    groups = rows.shape[0] // (SUBLANES * SPOTS)
    channels = parts * LANES
    tall = 32

    @pl.when(step == 0)
    def _():
        gain = [gain_ref[:, c * LANES : (c + 1) * LANES] for c in range(parts)]

        def norm(i, sums):
            at = pl.ds(pl.multiple_of(i * tall, tall), tall)
            inv = inv_ref[at, :]
            scaled = []
            new = []
            for c in range(parts):
                lanes = slice(c * LANES, (c + 1) * LANES)
                gn = gn_ref[at, lanes] + gn_other_ref[at, lanes].astype(F32)
                std = std_ref[at, lanes]
                product = gn * std
                gain_sum, shift_sum = sums[2 * c], sums[2 * c + 1]
                for r in range(0, tall, SUBLANES):
                    gain_sum = gain_sum + product[r : r + SUBLANES]
                    shift_sum = shift_sum + gn[r : r + SUBLANES]
                new += [gain_sum, shift_sum]
                scaled.append((gn * gain[c], product * gain[c], std))
            mean = sum(jnp.sum(v[0], axis=1, keepdims=True) for v in scaled) / channels
            mean_std = sum(jnp.sum(v[1], axis=1, keepdims=True) for v in scaled) / channels
            for c, (v, _, std) in enumerate(scaled):
                grad_conv[c, at, :] = inv * (v - mean - std * mean_std)
            return tuple(new)

        zero = jnp.zeros((SUBLANES, LANES), F32)
        sums = lax.fori_loop(0, slots * SPOTS // tall, norm, (zero,) * (2 * parts))
        for c in range(parts):
            lanes = slice(c * LANES, (c + 1) * LANES)
            channel_ref[0:1, lanes] = jnp.sum(sums[2 * c], axis=0, keepdims=True)
            channel_ref[1:2, lanes] = jnp.sum(sums[2 * c + 1], axis=0, keepdims=True)
        pad = groups * SUBLANES * SPOTS - slots * SPOTS
        if pad:
            for c in range(parts):
                grad_conv[c, slots * SPOTS :, :] = jnp.zeros((pad, LANES), F32)
            rows[slots * SPOTS :, :] = jnp.zeros((pad, LANES), F32)

    spread_taps(taps_ref, spread)

    def load(slot, _):
        rows[pl.ds(pl.multiple_of(slot * SPOTS, SPOTS), SPOTS), :] = (
            x_ref[slot].astype(F32).reshape(SPOTS, LANES)
        )
        return 0

    lax.fori_loop(0, slots, load, 0)
    to_patch_minor(rows, minor, groups)
    to_patch_minor(grad_conv.at[step], grad_minor, groups)

    def convolve(group, _):
        def emit(spot, value):
            result[pl.ds(group * SUBLANES * SPOTS + spot, SUBLANES, stride=SPOTS), :] = value

        conv_rows(grad_minor, spread, group, True, emit)
        return 0

    lax.fori_loop(0, groups, convolve, 0)

    def taps(group, _):
        for a in range(TAPS):
            sums = [
                jnp.where(group == 0, 0.0, tap_sums[a * TAPS + b]) for b in range(TAPS)
            ]
            for p in range(SIDE):
                row = p + a - REACH
                if not 0 <= row < SIDE:
                    continue
                values = [minor[group * SPOTS + row * SIDE + q] for q in range(SIDE)]
                grads = [grad_minor[group * SPOTS + p * SIDE + q] for q in range(SIDE)]
                for b in range(TAPS):
                    for q in range(SIDE):
                        col = q + b - REACH
                        if 0 <= col < SIDE:
                            sums[b] = sums[b] + grads[q] * values[col]
            for b in range(TAPS):
                tap_sums[a * TAPS + b] = sums[b]
        return 0

    lax.fori_loop(0, groups, taps, 0)
    for tap in range(TAPS * TAPS):
        grad_taps_ref[tap : tap + 1, :] = jnp.sum(tap_sums[tap], axis=0, keepdims=True)

    count = count_ref[0, 0]

    def finish(slot, _):
        live = jnp.where(slot < count, 1.0, 0.0)
        g = g_ref[slot].astype(F32) * live
        at = pl.ds(pl.multiple_of(slot * SPOTS, SPOTS), SPOTS)
        in_grad_ref[slot] = g + result[at, :].reshape(SIDE, SIDE, LANES)
        return 0

    lax.fori_loop(0, slots, finish, 0)


def backward(x, g, count, taps, gain, std, inv, grad_normed, grad_other):
    slots, channels = x.shape[0], x.shape[3]
    tokens, parts = slots * SPOTS, channels // LANES
    groups = -(-slots // SUBLANES)
    padded = groups * SUBLANES * SPOTS
    return pl.pallas_call(
        functools.partial(backward_kernel, slots),
        grid=(parts,),
        in_specs=[
            pl.BlockSpec((slots, SIDE, SIDE, LANES), lambda j: (0, 0, 0, j)),
            pl.BlockSpec((slots, SIDE, SIDE, LANES), lambda j: (0, 0, 0, j)),
            pl.BlockSpec(memory_space=pltpu.SMEM),
            pl.BlockSpec((TAPS * TAPS, LANES), lambda j: (0, j)),
            whole((1, channels)),
            whole((tokens, channels)),
            whole((tokens, 1)),
            whole((tokens, channels)),
            whole((tokens, channels)),
        ],
        out_specs=[
            pl.BlockSpec((slots, SIDE, SIDE, LANES), lambda j: (0, 0, 0, j)),
            pl.BlockSpec((TAPS * TAPS, LANES), lambda j: (0, j)),
            whole((2, channels)),
        ],
        out_shape=[
            jax.ShapeDtypeStruct((slots, SIDE, SIDE, channels), F32),
            jax.ShapeDtypeStruct((TAPS * TAPS, channels), F32),
            jax.ShapeDtypeStruct((2, channels), F32),
        ],
        scratch_shapes=[
            pltpu.VMEM((padded, LANES), F32),
            pltpu.VMEM((groups * SPOTS, SUBLANES, LANES), F32),
            pltpu.VMEM((groups * SPOTS, SUBLANES, LANES), F32),
            pltpu.VMEM((TAPS * TAPS, SUBLANES, LANES), F32),
            pltpu.VMEM((parts, padded, LANES), F32),
            pltpu.VMEM((padded, LANES), F32),
            pltpu.VMEM((TAPS * TAPS, SUBLANES, LANES), F32),
        ],
        compiler_params=pltpu.CompilerParams(vmem_limit_bytes=VMEM_LIMIT),
        cost_estimate=pl.CostEstimate(
            flops=4 * 49 * tokens * channels, bytes_accessed=16 * tokens * channels, transcendentals=0
        ),
        name="backward",
    )(x, g, count, taps, gain, std, inv, grad_normed, grad_other)


def device_index(x, y, z, core):
    high, low = divmod(y % Y, 2)
    return ((x % X) * 4 + high * 2 + core) * (2 * Z) + (z % Z) * 2 + low


def move(value, dy=0, dz=0, flip=0):
    pairs = [
        (device_index(x, y, z, core), device_index(x, y + dy, z + dz, core ^ flip))
        for x in range(X)
        for y in range(Y)
        for z in range(Z)
        for core in range(2)
    ]
    return lax.ppermute(value, AXES, pairs)


def gather_pieces(piece, z, low):
    half = Z // 2
    ahead, behind = [piece], []
    right = left = piece
    up, down = [], []
    for step in range(half):
        up.append(move(right, dy=1))
        right = move(right, dz=1)
        if step < half - 1:
            ahead.append(right)
            left = move(left, dz=-1)
            behind.append(left)
        else:
            behind.append(right)
        down.append(move(behind[-1], dy=-1))
    order, pieces = [], []
    for parity, (back, forth) in enumerate(((ahead, behind), (up, down))):
        for step in range(half):
            pieces += [back[step], forth[step]]
            order += [
                (z + Z - step) % Z * 2 + (low ^ parity),
                (z + 1 + step) % Z * 2 + (low ^ parity),
            ]
    return jnp.stack(order).astype(jnp.int32), pieces


def scatter_sums(first, second, z, low):
    def term(parity, offsets):
        at = [(z + s) % Z * 2 + (low ^ parity) for s in offsets]
        return jnp.stack(
            [
                jnp.concatenate(
                    [
                        lax.dynamic_index_in_dim(first, f, 0, keepdims=False),
                        lax.dynamic_index_in_dim(second, f, 0, keepdims=False),
                    ]
                )
                for f in at
            ]
        )

    up = [move(term(1, (4, 3)), dy=1)]
    down = [move(term(1, (5, 6)), dy=-1)]
    up.append(move(term(1, (2, 1)), dy=1))
    down.append(move(term(1, (7, 0)), dy=-1))

    def total(s, passing=None):
        batch, i = ((up, 4 - s) if 1 <= s <= 4 else (down, s - 5 if s else 3))
        out = term(0, (s,))[0].astype(F32) + batch[i // 2][i % 2].astype(F32)
        return out if passing is None else out + passing.astype(F32)

    right = move(total(4).astype(BF16), dz=1)
    left = move(total(5).astype(BF16), dz=-1)
    right = move(total(3, right).astype(BF16), dz=1)
    left = move(total(6, left).astype(BF16), dz=-1)
    right = move(total(2, right).astype(BF16), dz=1)
    left = move(total(7, left).astype(BF16), dz=-1)
    right = move(total(1, right).astype(BF16), dz=1)
    return total(0, left) + right.astype(F32)


def local(
    patches,
    out_grad,
    row_counts,
    dw_kernel,
    ln_gain,
    ln_bias,
    w_first,
    first_bias,
    w_second,
    layer_scale,
):
    fsdp, dp = lax.axis_size("fsdp"), lax.axis_size("dp")
    own = ln_gain.shape[0]
    units = first_bias.shape[0]
    channels, hidden = own * fsdp, units * fsdp
    mine = hidden // 2
    tap_count = dw_kernel.shape[0]
    dp_index, fsdp_index = lax.axis_index("dp"), lax.axis_index("fsdp")
    core = dp_index % 2
    z, low = fsdp_index // 2, fsdp_index % 2

    small = jnp.concatenate(
        [dw_kernel.reshape(-1), ln_gain, ln_bias, layer_scale, first_bias]
    )[None]
    small = lax.all_to_all(
        jnp.broadcast_to(small, (fsdp, small.shape[1])), "fsdp", 0, 0, tiled=True
    )
    cut = tap_count * own
    taps = small[:, :cut].reshape(fsdp, tap_count, own).transpose(1, 0, 2)
    taps = taps.reshape(tap_count, channels).astype(F32)
    gain, shift, scale = (
        small[:, cut + i * own : cut + (i + 1) * own].reshape(1, channels).astype(F32)
        for i in range(3)
    )
    bias = small[:, cut + 3 * own :].reshape(1, hidden).astype(F32)
    bias = lax.dynamic_slice_in_dim(bias, core * mine, mine, 1)

    part = lax.dynamic_slice_in_dim(w_first, core * mine, mine, 1)
    part = [part[:, k * CUT : (k + 1) * CUT] for k in range(mine // CUT)]
    part.append(lax.dynamic_slice_in_dim(w_second, core * CUT, CUT, 1))
    order, pieces = gather_pieces(jnp.concatenate(part), z, low)
    kept = mine // CUT * own
    wanted = jnp.arange(fsdp // 2, dtype=jnp.int32) + (1 - core) * (fsdp // 2)
    away = (wanted // 2 - z + Z) % Z
    wanted = (wanted % 2 ^ low) * Z + jnp.where(
        (away >= 1) & (away <= Z // 2), 2 * away - 1, (Z - away) % Z * 2
    )
    second = jnp.take(jnp.stack([piece[kept:] for piece in pieces]), wanted, axis=0)
    second = move(second, flip=1)

    x, g = patches[0], out_grad[0]
    normed, std, inv, gb = forward(x, g, row_counts, taps, gain, shift, scale)
    normed_other, gb_other = move(normed, flip=1), move(gb, flip=1)
    grad_first, second_mine, second_theirs, gn_mine, gn_theirs, grad_bias, scale_sum = mlp(
        core.reshape(1), order, normed, normed_other, gb, gb_other, bias, second, pieces
    )
    received = move(second_theirs, flip=1)
    grad_second = jnp.where(
        core == 0,
        jnp.concatenate([second_mine, received]),
        jnp.concatenate([received, second_mine]),
    )
    gn_other = move(gn_theirs, flip=1)
    scale_sum = scale_sum / scale
    in_grad, grad_taps, channel_sums = backward(
        x, g, row_counts, taps, gain, std, inv, gn_mine, gn_other
    )
    weights = scatter_sums(grad_first, grad_second, z, low)

    sums = jnp.concatenate([grad_taps, channel_sums, scale_sum], axis=0)
    lines = sums.shape[0]
    sums = sums.reshape(lines, fsdp, own).transpose(1, 0, 2).reshape(fsdp, lines * own)
    grad_bias = jnp.concatenate([grad_bias, grad_bias], axis=1).reshape(fsdp, units)
    computed = (jnp.arange(fsdp, dtype=jnp.int32) // (fsdp // 2) == core)[:, None]
    sums = jnp.concatenate([sums, jnp.where(computed, grad_bias, 0.0)], axis=1)
    sums = lax.all_to_all(sums, "fsdp", 0, 0, tiled=True)
    sums = jnp.sum(sums, axis=0)
    size = sums.shape[0]

    chips = dp // 2
    padded = -(-size // (chips * CUT)) * CUT
    sums = jnp.pad(sums, (0, chips * padded - size)).reshape(chips, padded // CUT, CUT)
    rows = weights.shape[0] // chips
    terms = jnp.concatenate([weights.reshape(chips, rows, CUT), sums], axis=1)
    same_core = [[2 * i + c for i in range(chips)] for c in range(2)]
    terms = lax.all_to_all(terms, "dp", 0, 0, tiled=True, axis_index_groups=same_core)
    factor = 1.0 / math.sqrt(fsdp * dp * ROWS * SPOTS)
    terms = jnp.sum(terms, axis=0) * factor
    terms = lax.all_to_all(
        jnp.broadcast_to(terms[None], (dp,) + terms.shape), "dp", 0, 0, tiled=True
    )
    terms = terms.reshape(chips, 2, terms.shape[1], CUT).transpose(1, 0, 2, 3)
    sums = (terms[0, :, rows:] + terms[1, :, rows:]).reshape(-1)
    weights = terms[:, :, :rows].reshape(2, chips * rows, CUT)
    first = weights[:, :kept].reshape(2, mine // CUT, own, CUT).transpose(2, 0, 1, 3)
    split = sums[: lines * own].reshape(lines, own)
    return (
        in_grad[None],
        first.reshape(own, hidden),
        weights[:, kept:].transpose(1, 0, 2).reshape(units, channels),
        split[:tap_count],
        sums[lines * own : size],
        split[tap_count:],
    )


def solution(mesh):
    placed = (
        P("fsdp", "dp", None, None, None),
        P("fsdp", "dp", None, None, None),
        P("fsdp", "dp"),
        P(None, "fsdp"),
        P("fsdp"),
        P("fsdp"),
        P("fsdp", None),
        P("fsdp"),
        P("fsdp", None),
        P("fsdp"),
    )
    return jax.shard_map(
        local,
        mesh=mesh,
        in_specs=placed,
        out_specs=(
            P("fsdp", "dp", None, None, None),
            P("fsdp", None),
            P("fsdp", None),
            P(None, "fsdp"),
            P("fsdp"),
            P(None, "fsdp"),
        ),
        check_vma=False,
    )
```

```python
import functools
import math

import jax
import jax.numpy as jnp
from jax import lax
from jax.experimental import pallas as pl
from jax.experimental.pallas import tpu as pltpu
from jax.sharding import PartitionSpec as P

ROWS = 8
LANES = 128
SUBLANES = 8
SIDE = 8
SPOTS = SIDE * SIDE
REACH = 3
TAPS = 7
BLOCK = 384
TOKEN_BLOCK = 448
NORM_BLOCK = 128
PART_TILES = 7
GROUP_STEPS = 2
CUT = 384
AXES = ("dp", "fsdp")
X, Y, Z = 4, 4, 8
BF16, F32 = jnp.bfloat16, jnp.float32
VMEM_LIMIT = 56 * 1024 * 1024
SMALL_VMEM = 24 * 1024 * 1024


def whole(shape):
    return pl.BlockSpec(shape, lambda *_: (0,) * len(shape))


def spread_taps(taps_ref, spread):
    for tap in range(TAPS * TAPS):
        spread[tap] = jnp.broadcast_to(taps_ref[tap : tap + 1, :], (SUBLANES, LANES))


def to_patch_minor(rows, out, groups):
    def one(spot, _):
        for group in range(groups):
            out[group * SPOTS + spot] = rows[
                pl.ds(group * SUBLANES * SPOTS + spot, SUBLANES, stride=SPOTS), :
            ]
        return 0

    lax.fori_loop(0, SPOTS, one, 0, unroll=8)


def conv_rows(src, spread, group, flip, emit):
    for p in range(SIDE):
        sums = [None] * SIDE
        for a in range(TAPS):
            row = p + a - REACH
            if not 0 <= row < SIDE:
                continue
            values = [src[group * SPOTS + row * SIDE + q] for q in range(SIDE)]
            for b in range(TAPS):
                tap = a * TAPS + b
                weight = spread[TAPS * TAPS - 1 - tap if flip else tap]
                for q in range(SIDE):
                    col = q + b - REACH
                    if 0 <= col < SIDE:
                        term = values[col] * weight
                        sums[q] = term if sums[q] is None else sums[q] + term
        for q in range(SIDE):
            emit(p * SIDE + q, sums[q])


def conv_kernel(
    slots, x_ref, taps_ref, _after, _buffer, out_ref, rows, minor, spread, conv
):
    groups = rows.shape[0] // (SUBLANES * SPOTS)
    spread_taps(taps_ref, spread)

    def load(slot, _):
        rows[pl.ds(pl.multiple_of(slot * SPOTS, SPOTS), SPOTS), :] = (
            x_ref[slot].astype(F32).reshape(SPOTS, LANES)
        )
        return 0

    lax.fori_loop(0, slots, load, 0)
    to_patch_minor(rows, minor, groups)

    def convolve(group, _):
        def emit(spot, value):
            conv[pl.ds(group * SUBLANES * SPOTS + spot, SUBLANES, stride=SPOTS), :] = value

        conv_rows(minor, spread, group, False, emit)
        return 0

    lax.fori_loop(0, groups, convolve, 0)
    out_ref[...] = conv[: slots * SPOTS, :]


def shapes_of(x):
    slots, channels = x.shape[0], x.shape[3]
    groups = -(-slots // SUBLANES)
    return slots, channels, slots * SPOTS, groups, groups * SUBLANES * SPOTS


def conv_part(part, x, taps, after, buffer):
    slots, channels, tokens, groups, padded = shapes_of(x)
    base = part * GROUP_STEPS
    anywhere = pl.BlockSpec(memory_space=pl.ANY)
    if buffer is None:
        buffer, aliases = after, {}
    else:
        aliases = {3: 0}
    return pl.pallas_call(
        functools.partial(conv_kernel, slots),
        grid=(GROUP_STEPS,),
        in_specs=[
            pl.BlockSpec((slots, SIDE, SIDE, LANES), lambda j: (0, 0, 0, j + base)),
            pl.BlockSpec((TAPS * TAPS, LANES), lambda j: (0, j + base)),
            anywhere,
            anywhere,
        ],
        out_specs=pl.BlockSpec((tokens, LANES), lambda j: (0, j + base)),
        out_shape=jax.ShapeDtypeStruct((tokens, channels), F32),
        input_output_aliases=aliases,
        scratch_shapes=[
            pltpu.VMEM((padded, LANES), F32),
            pltpu.VMEM((groups * SPOTS, SUBLANES, LANES), F32),
            pltpu.VMEM((TAPS * TAPS, SUBLANES, LANES), F32),
            pltpu.VMEM((padded, LANES), F32),
        ],
        compiler_params=pltpu.CompilerParams(vmem_limit_bytes=SMALL_VMEM),
        cost_estimate=pl.CostEstimate(
            flops=2 * 49 * tokens * LANES * GROUP_STEPS,
            bytes_accessed=6 * tokens * LANES * GROUP_STEPS,
            transcendentals=0,
        ),
        name="conv",
    )(x, taps, after, buffer)


def norm_kernel(
    conv_ref, g_ref, count_ref, gain_ref, shift_ref, scale_ref, _after,
    normed_ref, std_ref, inv_ref, gb_ref,
):
    step = pl.program_id(0)
    count = count_ref[0, 0]
    channels = conv_ref.shape[1]
    parts = [slice(c, c + LANES) for c in range(0, channels, LANES)]
    gain, shift, scale = ([ref[:, c] for c in parts] for ref in (gain_ref, shift_ref, scale_ref))
    tall = 32

    def norm(i, _):
        at = pl.ds(pl.multiple_of(i * tall, tall), tall)
        values = [conv_ref[at, c] for c in parts]
        mean = sum(jnp.sum(v, axis=1, keepdims=True) for v in values) / channels
        values = [v - mean for v in values]
        var = sum(jnp.sum(v * v, axis=1, keepdims=True) for v in values) / channels
        inv = lax.rsqrt(var + 1e-06)
        inv_ref[at, :] = inv
        for c, v in enumerate(values):
            std = v * inv
            std_ref[at, parts[c]] = std
            normed_ref[at, parts[c]] = (std * gain[c] + shift[c]).astype(BF16)
        return 0

    lax.fori_loop(0, NORM_BLOCK // tall, norm, 0, unroll=2)
    for slot in range(NORM_BLOCK // SPOTS):
        live = jnp.where(step * (NORM_BLOCK // SPOTS) + slot < count, 1.0, 0.0)
        for c, lanes in enumerate(parts):
            g = g_ref[slot, :, :, lanes].astype(F32).reshape(SPOTS, LANES)
            gb_ref[slot * SPOTS : (slot + 1) * SPOTS, lanes] = (g * (scale[c] * live)).astype(BF16)


def norm(conv, g, count, gain, shift, scale, after):
    tokens, channels = conv.shape
    block = pl.BlockSpec((NORM_BLOCK, channels), lambda j: (j, 0))
    vector = whole((1, channels))
    return pl.pallas_call(
        norm_kernel,
        grid=(tokens // NORM_BLOCK,),
        in_specs=[
            block,
            pl.BlockSpec((NORM_BLOCK // SPOTS, SIDE, SIDE, channels), lambda j: (j, 0, 0, 0)),
            pl.BlockSpec(memory_space=pltpu.SMEM),
            vector, vector, vector,
            pl.BlockSpec(memory_space=pl.ANY),
        ],
        out_specs=[block, block, pl.BlockSpec((NORM_BLOCK, 1), lambda j: (j, 0)), block],
        out_shape=[
            jax.ShapeDtypeStruct((tokens, channels), BF16),
            jax.ShapeDtypeStruct((tokens, channels), F32),
            jax.ShapeDtypeStruct((tokens, 1), F32),
            jax.ShapeDtypeStruct((tokens, channels), BF16),
        ],
        compiler_params=pltpu.CompilerParams(vmem_limit_bytes=SMALL_VMEM),
        cost_estimate=pl.CostEstimate(
            flops=20 * tokens * channels, bytes_accessed=14 * tokens * channels, transcendentals=0
        ),
        name="norm",
    )(conv, g, count, gain, shift, scale, after)


def tile_of(part, i, across):
    return divmod(part * PART_TILES + i, across)


def mlp_kernel(
    count, core_ref, order_ref, mine_ref, theirs_ref, gb_mine_ref, gb_theirs_ref, bias_ref,
    second_ref, *refs,
):
    pieces = refs[:count]
    (
        sums_ref, gn_mine_ref, gn_theirs_ref, grad_bias_ref, scale_ref,
        first, second, sum_first, sum_second, tokens, cots, flipped, grad_normed, sems,
    ) = refs[count:]
    step = pl.program_id(0)
    steps = pl.num_programs(0)
    channels, hidden = first.shape
    chips = second_ref.shape[0]
    cuts = hidden // CUT
    own = pieces[0].shape[0] // (2 * cuts)
    shards = channels // own
    units = hidden // (shards // 2)
    first_rows = shards * PART_TILES * SUBLANES
    part_rows = PART_TILES * 2 * SUBLANES
    tall = 2 * SUBLANES
    dot = functools.partial(lax.dot_general, preferred_element_type=F32)

    def aligned(value, to):
        return pl.multiple_of(value * to, to)

    @pl.when(step == 0)
    def _():
        made = []
        for i, piece in enumerate(pieces):
            for parity in range(2):
                f = order_ref[2 * i + parity]
                for k in range(cuts):
                    made.append(
                        pltpu.make_async_copy(
                            piece.at[pl.ds((parity * cuts + k) * own, own), :],
                            first.at[pl.ds(aligned(f, own), own), pl.ds(k * CUT, CUT)],
                            sems.at[i],
                        )
                    )
        for copy in made:
            copy.start()

        def unpack_shard(f, _):
            for e in range(chips):
                for i in range(PART_TILES):
                    r, c = tile_of(e, i, channels // LANES)
                    if r * tall < units:
                        second[
                            pl.ds(pl.multiple_of(f * units + r * tall, tall), tall),
                            c * LANES : (c + 1) * LANES,
                        ] = second_ref[
                            e, pl.ds(pl.multiple_of(f * part_rows + i * tall, tall), tall), :
                        ]
            return 0

        lax.fori_loop(0, shards // 2, unpack_shard, 0)
        scale_ref[...] = jnp.zeros_like(scale_ref)
        grad_bias_ref[...] = jnp.zeros_like(grad_bias_ref)

        def clear(i, _):
            sum_first[pl.ds(aligned(i, tall), tall), :] = jnp.zeros((tall, hidden), F32)
            return 0

        lax.fori_loop(0, channels // tall, clear, 0)

        def clear_more(i, _):
            sum_second[pl.ds(aligned(i, tall), tall), :] = jnp.zeros((tall, channels), F32)
            return 0

        lax.fori_loop(0, hidden // tall, clear_more, 0)
        for copy in made:
            copy.wait()

    @pl.when(step < steps // 2)
    def _():
        tokens[...] = mine_ref[...]
        cots[...] = gb_mine_ref[...]

    @pl.when(step >= steps // 2)
    def _():
        tokens[...] = theirs_ref[...]
        cots[...] = gb_theirs_ref[...]

    flipped[...] = tokens[...].T
    grad_normed[...] = jnp.zeros_like(grad_normed)

    def chunk(h, _):
        at = pl.ds(aligned(h, BLOCK), BLOCK)
        normed, gb = tokens[...], cots[...]
        preact = dot(normed, first[:, at], (((1,), (0,)), ((), ()))) + bias_ref[:, at]
        grad_hidden = dot(gb, second[at, :], (((1,), (1,)), ((), ())))
        prob = 0.5 * (1.0 + lax.erf(preact * 0.7071067811865476))
        active = (preact * prob).astype(BF16)
        slope = prob + preact * jnp.exp(-0.5 * preact * preact) * 0.3989422804014327
        grad_preact = (grad_hidden * slope).astype(BF16)
        sum_second[at, :] += dot(active, gb, (((0,), (0,)), ((), ())))
        sum_first[:, at] += dot(flipped[...], grad_preact, (((1,), (0,)), ((), ())))
        grad_bias_ref[:, at] += jnp.sum(grad_preact.astype(F32), axis=0, keepdims=True)
        grad_normed[...] += dot(grad_preact, first[:, at], (((1,), (1,)), ((), ())))
        return 0

    lax.fori_loop(0, hidden // BLOCK, chunk, 0)

    @pl.when(step < steps // 2)
    def _():
        gn_mine_ref[...] = grad_normed[...]

    @pl.when(step >= steps // 2)
    def _():
        gn_theirs_ref[...] = grad_normed[...].astype(BF16)

    @pl.when(step == steps - 1)
    def _():
        def scale_rows(i, total):
            at = pl.ds(aligned(i, tall), tall)
            return total + sum_second[at, :] * second[at, :].astype(F32)

        total = lax.fori_loop(
            0, hidden // tall, scale_rows, jnp.zeros((tall, channels), F32)
        )
        scale_ref[...] = jnp.sum(total, axis=0, keepdims=True)
        none = jnp.zeros((SUBLANES, LANES), F32)

        def pack_pair(pair, _):
            for e in range(chips):
                tiles = []
                for f in range(2):
                    for i in range(PART_TILES):
                        r, c = tile_of(e, i, hidden // LANES)
                        row = pl.multiple_of((2 * pair + f) * own + r * SUBLANES, SUBLANES)
                        tiles.append(
                            sum_first[pl.ds(row, SUBLANES), c * LANES : (c + 1) * LANES]
                            if r * SUBLANES < own
                            else none
                        )
                for i in range(0, len(tiles), 2):
                    at = pl.multiple_of(pair * part_rows + i * SUBLANES, tall)
                    sums_ref[e, pl.ds(at, tall), :] = jnp.concatenate(tiles[i : i + 2]).astype(BF16)
            return 0

        lax.fori_loop(0, shards // 2, pack_pair, 0)

        def pack_shard(f, _):
            for e in range(chips):
                for i in range(PART_TILES):
                    r, c = tile_of(e, i, channels // LANES)
                    at = pl.multiple_of(first_rows + f * part_rows + i * tall, tall)
                    if r * tall < units:
                        row = pl.multiple_of(f * units + r * tall, tall)
                        value = sum_second[pl.ds(row, tall), c * LANES : (c + 1) * LANES]
                    else:
                        value = jnp.zeros((tall, LANES), F32)
                    sums_ref[e, pl.ds(at, tall), :] = value.astype(BF16)
            return 0

        lax.fori_loop(0, shards // 2, pack_shard, 0)


def mlp(core, order, mine, theirs, gb_mine, gb_theirs, bias, second, pieces):
    tokens, channels = mine.shape
    count = len(pieces)
    shards = 2 * count
    hidden = bias.shape[1]
    sums = (second.shape[0], shards * PART_TILES * SUBLANES + second.shape[1], LANES)
    steps = tokens // TOKEN_BLOCK
    early = pl.BlockSpec((TOKEN_BLOCK, channels), lambda j: (jnp.minimum(j, steps - 1), 0))
    late = pl.BlockSpec((TOKEN_BLOCK, channels), lambda j: (jnp.maximum(j - steps, 0), 0))
    anywhere = pl.BlockSpec(memory_space=pl.ANY)
    return pl.pallas_call(
        functools.partial(mlp_kernel, count),
        grid=(2 * steps,),
        in_specs=[
            pl.BlockSpec(memory_space=pltpu.SMEM),
            pl.BlockSpec(memory_space=pltpu.SMEM),
            early, late, early, late,
            whole((1, hidden)),
            whole(second.shape),
        ]
        + [anywhere] * count,
        out_specs=[
            whole(sums),
            early, late,
            whole((1, hidden)),
            whole((1, channels)),
        ],
        out_shape=[
            jax.ShapeDtypeStruct(sums, BF16),
            jax.ShapeDtypeStruct((tokens, channels), F32),
            jax.ShapeDtypeStruct((tokens, channels), BF16),
            jax.ShapeDtypeStruct((1, hidden), F32),
            jax.ShapeDtypeStruct((1, channels), F32),
        ],
        scratch_shapes=[
            pltpu.VMEM((channels, hidden), BF16),
            pltpu.VMEM((hidden, channels), BF16),
            pltpu.VMEM((channels, hidden), F32),
            pltpu.VMEM((hidden, channels), F32),
            pltpu.VMEM((TOKEN_BLOCK, channels), BF16),
            pltpu.VMEM((TOKEN_BLOCK, channels), BF16),
            pltpu.VMEM((channels, TOKEN_BLOCK), BF16),
            pltpu.VMEM((TOKEN_BLOCK, channels), F32),
            pltpu.SemaphoreType.DMA((count,)),
        ],
        compiler_params=pltpu.CompilerParams(vmem_limit_bytes=VMEM_LIMIT),
        cost_estimate=pl.CostEstimate(
            flops=20 * tokens * channels * hidden,
            bytes_accessed=12 * hidden * channels,
            transcendentals=4 * tokens * hidden,
        ),
        name="mlp",
    )(core, order, mine, theirs, gb_mine, gb_theirs, bias, second, *pieces)


def unnorm_kernel(gn_ref, gn_other_ref, std_ref, inv_ref, gain_ref, grad_conv_ref, channel_ref):
    step = pl.program_id(0)
    channels = gn_ref.shape[1]
    parts = [slice(c, c + LANES) for c in range(0, channels, LANES)]
    gain = [gain_ref[:, c] for c in parts]
    tall = 32

    @pl.when(step == 0)
    def _():
        channel_ref[...] = jnp.zeros_like(channel_ref)

    def one(i, sums):
        at = pl.ds(pl.multiple_of(i * tall, tall), tall)
        inv = inv_ref[at, :]
        scaled, new = [], []
        for c, lanes in enumerate(parts):
            gn = gn_ref[at, lanes] + gn_other_ref[at, lanes].astype(F32)
            std = std_ref[at, lanes]
            product = gn * std
            gain_sum, shift_sum = sums[2 * c], sums[2 * c + 1]
            for r in range(0, tall, SUBLANES):
                gain_sum = gain_sum + product[r : r + SUBLANES]
                shift_sum = shift_sum + gn[r : r + SUBLANES]
            new += [gain_sum, shift_sum]
            scaled.append((gn * gain[c], product * gain[c], std))
        mean = sum(jnp.sum(v[0], axis=1, keepdims=True) for v in scaled) / channels
        mean_std = sum(jnp.sum(v[1], axis=1, keepdims=True) for v in scaled) / channels
        for c, (v, _, std) in enumerate(scaled):
            grad_conv_ref[at, parts[c]] = inv * (v - mean - std * mean_std)
        return tuple(new)

    zero = jnp.zeros((SUBLANES, LANES), F32)
    sums = lax.fori_loop(0, NORM_BLOCK // tall, one, (zero,) * (2 * len(parts)))
    for c, lanes in enumerate(parts):
        channel_ref[0:1, lanes] += jnp.sum(sums[2 * c], axis=0, keepdims=True)
        channel_ref[1:2, lanes] += jnp.sum(sums[2 * c + 1], axis=0, keepdims=True)


def unnorm(gn, gn_other, std, inv, gain):
    tokens, channels = gn.shape
    block = pl.BlockSpec((NORM_BLOCK, channels), lambda j: (j, 0))
    return pl.pallas_call(
        unnorm_kernel,
        grid=(tokens // NORM_BLOCK,),
        in_specs=[
            block, block, block,
            pl.BlockSpec((NORM_BLOCK, 1), lambda j: (j, 0)),
            whole((1, channels)),
        ],
        out_specs=[block, whole((2, channels))],
        out_shape=[
            jax.ShapeDtypeStruct((tokens, channels), F32),
            jax.ShapeDtypeStruct((2, channels), F32),
        ],
        compiler_params=pltpu.CompilerParams(vmem_limit_bytes=SMALL_VMEM),
        cost_estimate=pl.CostEstimate(
            flops=20 * tokens * channels, bytes_accessed=14 * tokens * channels, transcendentals=0
        ),
        name="unnorm",
    )(gn, gn_other, std, inv, gain)


def load_grads(grad_ref, rows, grad_minor, groups, tokens):
    rows[:tokens, :] = grad_ref[...]
    if rows.shape[0] > tokens:
        rows[tokens:, :] = jnp.zeros((rows.shape[0] - tokens, LANES), F32)
    to_patch_minor(rows, grad_minor, groups)


def taps_kernel(
    slots, x_ref, grad_ref, _after, _buffer, grad_taps_ref, rows, minor, grad_minor, tap_sums
):
    groups = rows.shape[0] // (SUBLANES * SPOTS)
    load_grads(grad_ref, rows, grad_minor, groups, slots * SPOTS)

    def load(slot, _):
        rows[pl.ds(pl.multiple_of(slot * SPOTS, SPOTS), SPOTS), :] = (
            x_ref[slot].astype(F32).reshape(SPOTS, LANES)
        )
        return 0

    lax.fori_loop(0, slots, load, 0)
    to_patch_minor(rows, minor, groups)

    def taps(group, _):
        for a in range(TAPS):
            sums = [jnp.where(group == 0, 0.0, tap_sums[a * TAPS + b]) for b in range(TAPS)]
            for p in range(SIDE):
                row = p + a - REACH
                if not 0 <= row < SIDE:
                    continue
                values = [minor[group * SPOTS + row * SIDE + q] for q in range(SIDE)]
                grads = [grad_minor[group * SPOTS + p * SIDE + q] for q in range(SIDE)]
                for b in range(TAPS):
                    for q in range(SIDE):
                        col = q + b - REACH
                        if 0 <= col < SIDE:
                            sums[b] = sums[b] + grads[q] * values[col]
            for b in range(TAPS):
                tap_sums[a * TAPS + b] = sums[b]
        return 0

    lax.fori_loop(0, groups, taps, 0)
    for tap in range(TAPS * TAPS):
        grad_taps_ref[tap : tap + 1, :] = jnp.sum(tap_sums[tap], axis=0, keepdims=True)


def taps_part(part, x, grad_conv, after, buffer):
    slots, channels, tokens, groups, padded = shapes_of(x)
    base = part * GROUP_STEPS
    anywhere = pl.BlockSpec(memory_space=pl.ANY)
    if buffer is None:
        buffer, aliases = after, {}
    else:
        aliases = {3: 0}
    return pl.pallas_call(
        functools.partial(taps_kernel, slots),
        grid=(GROUP_STEPS,),
        in_specs=[
            pl.BlockSpec((slots, SIDE, SIDE, LANES), lambda j: (0, 0, 0, j + base)),
            pl.BlockSpec((tokens, LANES), lambda j: (0, j + base)),
            anywhere,
            anywhere,
        ],
        out_specs=pl.BlockSpec((TAPS * TAPS, LANES), lambda j: (0, j + base)),
        out_shape=jax.ShapeDtypeStruct((TAPS * TAPS, channels), F32),
        input_output_aliases=aliases,
        scratch_shapes=[
            pltpu.VMEM((padded, LANES), F32),
            pltpu.VMEM((groups * SPOTS, SUBLANES, LANES), F32),
            pltpu.VMEM((groups * SPOTS, SUBLANES, LANES), F32),
            pltpu.VMEM((TAPS * TAPS, SUBLANES, LANES), F32),
        ],
        compiler_params=pltpu.CompilerParams(vmem_limit_bytes=SMALL_VMEM),
        cost_estimate=pl.CostEstimate(
            flops=2 * 49 * tokens * LANES * GROUP_STEPS,
            bytes_accessed=6 * tokens * LANES * GROUP_STEPS,
            transcendentals=0,
        ),
        name="taps",
    )(x, grad_conv, after, buffer)


def back_kernel(
    slots, g_ref, grad_ref, count_ref, taps_ref, _after, _buffer, in_grad_ref,
    rows, grad_minor, spread, result,
):
    groups = rows.shape[0] // (SUBLANES * SPOTS)
    spread_taps(taps_ref, spread)
    load_grads(grad_ref, rows, grad_minor, groups, slots * SPOTS)

    def convolve(group, _):
        def emit(spot, value):
            result[pl.ds(group * SUBLANES * SPOTS + spot, SUBLANES, stride=SPOTS), :] = value

        conv_rows(grad_minor, spread, group, True, emit)
        return 0

    lax.fori_loop(0, groups, convolve, 0)
    count = count_ref[0, 0]

    def finish(slot, _):
        live = jnp.where(slot < count, 1.0, 0.0)
        g = g_ref[slot].astype(F32) * live
        at = pl.ds(pl.multiple_of(slot * SPOTS, SPOTS), SPOTS)
        in_grad_ref[slot] = g + result[at, :].reshape(SIDE, SIDE, LANES)
        return 0

    lax.fori_loop(0, slots, finish, 0)


def back_part(part, g, grad_conv, count, taps, after, buffer):
    slots, channels, tokens, groups, padded = shapes_of(g)
    base = part * GROUP_STEPS
    anywhere = pl.BlockSpec(memory_space=pl.ANY)
    if buffer is None:
        buffer, aliases = after, {}
    else:
        aliases = {5: 0}
    return pl.pallas_call(
        functools.partial(back_kernel, slots),
        grid=(GROUP_STEPS,),
        in_specs=[
            pl.BlockSpec((slots, SIDE, SIDE, LANES), lambda j: (0, 0, 0, j + base)),
            pl.BlockSpec((tokens, LANES), lambda j: (0, j + base)),
            pl.BlockSpec(memory_space=pltpu.SMEM),
            pl.BlockSpec((TAPS * TAPS, LANES), lambda j: (0, j + base)),
            anywhere,
            anywhere,
        ],
        out_specs=pl.BlockSpec((slots, SIDE, SIDE, LANES), lambda j: (0, 0, 0, j + base)),
        out_shape=jax.ShapeDtypeStruct((slots, SIDE, SIDE, channels), F32),
        input_output_aliases=aliases,
        scratch_shapes=[
            pltpu.VMEM((padded, LANES), F32),
            pltpu.VMEM((groups * SPOTS, SUBLANES, LANES), F32),
            pltpu.VMEM((TAPS * TAPS, SUBLANES, LANES), F32),
            pltpu.VMEM((padded, LANES), F32),
        ],
        compiler_params=pltpu.CompilerParams(vmem_limit_bytes=SMALL_VMEM),
        cost_estimate=pl.CostEstimate(
            flops=2 * 49 * tokens * LANES * GROUP_STEPS,
            bytes_accessed=10 * tokens * LANES * GROUP_STEPS,
            transcendentals=0,
        ),
        name="back",
    )(g, grad_conv, count, taps, after, buffer)


def device_index(x, y, z, core):
    high, low = divmod(y % Y, 2)
    return ((x % X) * 4 + high * 2 + core) * (2 * Z) + (z % Z) * 2 + low


def move(value, dy=0, dz=0, flip=0):
    pairs = [
        (device_index(x, y, z, core), device_index(x, y + dy, z + dz, core ^ flip))
        for x in range(X)
        for y in range(Y)
        for z in range(Z)
        for core in range(2)
    ]
    return lax.ppermute(value, AXES, pairs)


def gather_pieces(piece, z, low):
    other = lax.ppermute(piece, "fsdp", [(i, i ^ 1) for i in range(2 * Z)])
    pair = jnp.concatenate([piece, other])
    right = left = pair
    pieces, away = [pair], [0]
    for step in range(1, Z // 2 + 1):
        right = move(right, dz=1)
        pieces.append(right)
        away.append(Z - step)
        if step < Z // 2:
            left = move(left, dz=-1)
            pieces.append(left)
            away.append(step)
    order = [(z + s) % Z * 2 + (low ^ parity) for s in away for parity in range(2)]
    return jnp.stack(order).astype(jnp.int32), pieces


def add_up_kernel(terms_ref, _after, out_ref):
    tall = 8 * SUBLANES

    def rows(i, _):
        at = pl.ds(pl.multiple_of(i * tall, tall), tall)
        total = terms_ref[0, at, :].astype(F32)
        for e in range(1, terms_ref.shape[0]):
            total = total + terms_ref[e, at, :].astype(F32)
        out_ref[at, :] = total.astype(BF16)
        return 0

    lax.fori_loop(0, terms_ref.shape[1] // tall, rows, 0, unroll=2)


def add_up(terms, after):
    return pl.pallas_call(
        add_up_kernel,
        in_specs=[
            pl.BlockSpec(memory_space=pltpu.VMEM),
            pl.BlockSpec(memory_space=pl.ANY),
        ],
        out_shape=jax.ShapeDtypeStruct(terms.shape[1:], BF16),
        compiler_params=pltpu.CompilerParams(vmem_limit_bytes=SMALL_VMEM),
        name="add_up",
    )(terms, after)


def finish_kernel(factor, side_ref, terms_ref, first_ref, second_ref, small_ref):
    side = side_ref[0]
    chips = terms_ref.shape[0] // 2
    small_rows = PART_TILES * 2 * SUBLANES
    half = small_rows // 2
    wide = first_ref.shape[1] // 2 // LANES
    small = None
    for e in range(chips):
        for core in range(2):
            part = terms_ref[2 * e + core, :small_rows, :].astype(F32) * factor
            for i in range(PART_TILES):
                r, c = tile_of(e, i, wide)
                if r * SUBLANES < first_ref.shape[0]:
                    lane = (core * wide + c) * LANES
                    first_ref[r * SUBLANES : (r + 1) * SUBLANES, lane : lane + LANES] = part[
                        i * SUBLANES : (i + 1) * SUBLANES
                    ]
            more = terms_ref[2 * e + core, small_rows:, :].astype(F32)
            small = more if small is None else small + more
        part = jnp.concatenate(
            [
                terms_ref[2 * e + core, :small_rows, :].astype(F32)[half:]
                for core in (side, 1 - side)
            ]
        )
        part = part * factor
        for i in range(PART_TILES):
            r, c = tile_of(e, i, second_ref.shape[1] // LANES)
            if r * 2 * SUBLANES < second_ref.shape[0]:
                second_ref[r * 2 * SUBLANES : (r + 1) * 2 * SUBLANES, c * LANES : (c + 1) * LANES] = (
                    part[i * 2 * SUBLANES : (i + 1) * 2 * SUBLANES]
                )
    small_ref[...] = small * factor


def finish(side, terms, first_shape, second_shape, factor):
    small = (terms.shape[1] - PART_TILES * 2 * SUBLANES, LANES)
    return pl.pallas_call(
        functools.partial(finish_kernel, factor),
        in_specs=[
            pl.BlockSpec(memory_space=pltpu.SMEM),
            pl.BlockSpec(memory_space=pltpu.VMEM),
        ],
        out_shape=[
            jax.ShapeDtypeStruct(first_shape, F32),
            jax.ShapeDtypeStruct(second_shape, F32),
            jax.ShapeDtypeStruct(small, F32),
        ],
        compiler_params=pltpu.CompilerParams(vmem_limit_bytes=SMALL_VMEM),
        name="finish",
    )(side, terms)


def pack(rows):
    count, width = rows.shape[-2:]
    half = -(-count // 2)
    lead = [(0, 0)] * (rows.ndim - 2)
    rows = jnp.pad(rows, lead + [(0, 2 * half - count), (0, 0)])
    rows = jnp.concatenate([rows[..., :half, :], rows[..., half:, :]], axis=-1)
    return jnp.pad(rows, lead + [(0, -half % (2 * SUBLANES)), (0, LANES - 2 * width)])


def unpack(packed, count, width):
    half = -(-count // 2)
    rows = [packed[..., :half, :width], packed[..., :half, width : 2 * width]]
    return jnp.concatenate(rows, axis=-2)[..., :count, :]


def local(
    patches,
    out_grad,
    row_counts,
    dw_kernel,
    ln_gain,
    ln_bias,
    w_first,
    first_bias,
    w_second,
    layer_scale,
):
    fsdp, dp = lax.axis_size("fsdp"), lax.axis_size("dp")
    own = ln_gain.shape[0]
    units = first_bias.shape[0]
    channels, hidden = own * fsdp, units * fsdp
    mine = hidden // 2
    tap_count = dw_kernel.shape[0]
    dp_index, fsdp_index = lax.axis_index("dp"), lax.axis_index("fsdp")
    core = dp_index % 2
    z, low = fsdp_index // 2, fsdp_index % 2

    chip, chips = dp_index // 2, dp // 2
    side = fsdp_index // (fsdp // 2)
    same_core = [[2 * i + c for i in range(chips)] for c in range(2)]
    flat = (PART_TILES * SUBLANES, LANES)

    tall, across = units // (2 * SUBLANES), channels // LANES
    tiles = w_second.reshape(tall, 2 * SUBLANES, across, LANES).transpose(0, 2, 1, 3)
    tiles = tiles.reshape(tall * across, 2 * SUBLANES, LANES)
    tiles = jnp.pad(tiles, ((0, chips * PART_TILES - tall * across), (0, 0), (0, 0)))
    tiles = tiles.reshape(chips * 2, *flat)
    tiles = lax.dynamic_index_in_dim(tiles, 2 * chip + (core ^ side), 0, keepdims=False)
    vectors = [ln_gain[None], ln_bias[None], layer_scale[None], first_bias.reshape(-1, own)]
    small = jnp.concatenate([dw_kernel] + vectors)
    lines = small.shape[0]
    small = jnp.concatenate([tiles, pack(small)])
    small = lax.all_to_all(
        jnp.broadcast_to(small, (fsdp,) + small.shape), "fsdp", 0, 0, tiled=True
    )
    tiles, small = small[:, : flat[0]], unpack(small[:, flat[0] :], lines, own)
    kept = lax.dynamic_slice_in_dim(tiles, core * (fsdp // 2), fsdp // 2)
    swapped = move(lax.dynamic_slice_in_dim(tiles, (1 - core) * (fsdp // 2), fsdp // 2), flip=1)
    second = jnp.concatenate([kept, swapped], axis=1).reshape(fsdp * flat[0], LANES)
    second = lax.all_to_all(
        jnp.broadcast_to(second, (chips,) + second.shape),
        "dp", 0, 0, tiled=True, axis_index_groups=same_core,
    )
    taps = small[:, :tap_count].transpose(1, 0, 2).reshape(tap_count, channels).astype(F32)
    gain, shift, scale = (
        small[:, tap_count + i].reshape(1, channels).astype(F32) for i in range(3)
    )
    bias = small[:, tap_count + 3 :].reshape(1, hidden).astype(F32)
    bias = lax.dynamic_slice_in_dim(bias, core * mine, mine, 1)

    part = lax.dynamic_slice_in_dim(w_first, core * mine, mine, 1)
    part = [part[:, k * CUT : (k + 1) * CUT] for k in range(mine // CUT)]
    order, pieces = gather_pieces(jnp.concatenate(part), z, low)

    x, g = patches[0], out_grad[0]
    conv = conv_part(0, x, taps, pieces[2], None)
    conv = conv_part(1, x, taps, pieces[4], conv)
    conv = conv_part(2, x, taps, pieces[5], conv)
    normed, std, inv, gb = norm(conv, g, row_counts, gain, shift, scale, pieces[6])
    normed_other, gb_other = move(normed, flip=1), move(gb, flip=1)
    terms, gn_mine, gn_theirs, grad_bias, scale_sum = mlp(
        core.reshape(1), order, normed, normed_other, gb, gb_other, bias, second, pieces
    )
    gn_other = move(gn_theirs, flip=1)
    scale_sum = scale_sum / scale
    grad_conv, channel_sums = unnorm(gn_mine, gn_other, std, inv, gain)
    grad_taps = taps_part(0, x, grad_conv, terms, None)
    grad_taps = taps_part(1, x, grad_conv, terms, grad_taps)
    grad_taps = taps_part(2, x, grad_conv, terms, grad_taps)
    in_grad = back_part(0, g, grad_conv, row_counts, taps, terms, None)
    in_grad = back_part(1, g, grad_conv, row_counts, taps, terms, in_grad)
    in_grad = back_part(2, g, grad_conv, row_counts, taps, terms, in_grad)

    terms = lax.all_to_all(terms, "dp", 0, 0, tiled=True, axis_index_groups=same_core)
    terms = add_up(terms, in_grad)
    first = terms[: fsdp * flat[0]].reshape((fsdp,) + flat)
    second = terms[fsdp * flat[0] :].reshape((fsdp // 2, 2) + flat)
    swapped = move(second[:, 1], flip=1)
    second = jnp.where(
        core == 0,
        jnp.concatenate([second[:, 0], swapped]),
        jnp.concatenate([swapped, second[:, 0]]),
    )
    sums = jnp.concatenate([grad_taps, channel_sums, scale_sum], axis=0)
    sums = sums.reshape(sums.shape[0], fsdp, own).transpose(1, 0, 2)
    grad_bias = jnp.concatenate([grad_bias, grad_bias], axis=1).reshape(fsdp, -1, own)
    computed = (jnp.arange(fsdp, dtype=jnp.int32) // (fsdp // 2) == core)[:, None, None]
    sums = jnp.concatenate([sums, jnp.where(computed, grad_bias, 0.0)], axis=1)
    terms = jnp.concatenate([first, second, pack(sums.astype(BF16))], axis=1)
    terms = lax.all_to_all(terms, "fsdp", 0, 0, tiled=True)
    terms = jnp.sum(terms.astype(F32), axis=0).astype(BF16)
    terms = lax.all_to_all(
        jnp.broadcast_to(terms[None], (dp,) + terms.shape), "dp", 0, 0, tiled=True
    )
    factor = 1.0 / math.sqrt(fsdp * dp * ROWS * SPOTS)
    first, second, sums = finish(
        side.reshape(1), terms, (own, hidden), (units, channels), factor
    )
    sums = unpack(sums, lines, own)
    return (
        in_grad[None],
        first,
        second,
        sums[:tap_count],
        sums[tap_count + 3 :].reshape(units),
        sums[tap_count : tap_count + 3],
    )


def solution(mesh):
    placed = (
        P("fsdp", "dp", None, None, None),
        P("fsdp", "dp", None, None, None),
        P("fsdp", "dp"),
        P(None, "fsdp"),
        P("fsdp"),
        P("fsdp"),
        P("fsdp", None),
        P("fsdp"),
        P("fsdp", None),
        P("fsdp"),
    )
    return jax.shard_map(
        local,
        mesh=mesh,
        in_specs=placed,
        out_specs=(
            P("fsdp", "dp", None, None, None),
            P("fsdp", None),
            P("fsdp", None),
            P(None, "fsdp"),
            P("fsdp"),
            P(None, "fsdp"),
        ),
        check_vma=False,
    )
```

```python
import functools
import math

import jax
import jax.numpy as jnp
from jax import lax
from jax.experimental import pallas as pl
from jax.experimental.pallas import tpu as pltpu
from jax.sharding import PartitionSpec as P

ROWS = 8
LANES = 128
SUBLANES = 8
SIDE = 8
SPOTS = SIDE * SIDE
REACH = 3
TAPS = 7
BLOCK = 256
NORM_BLOCK = 128
PART_TILES = 7
GROUP_STEPS = 2
CUT = 384
AXES = ("dp", "fsdp")
X, Y, Z = 4, 4, 8
BF16, F32 = jnp.bfloat16, jnp.float32
VMEM_LIMIT = 56 * 1024 * 1024
SMALL_VMEM = 24 * 1024 * 1024


def whole(shape):
    return pl.BlockSpec(shape, lambda *_: (0,) * len(shape))


def spread_taps(taps_ref, spread):
    for tap in range(TAPS * TAPS):
        spread[tap] = jnp.broadcast_to(taps_ref[tap : tap + 1, :], (SUBLANES, LANES))


def to_patch_minor(rows, out, groups):
    def one(spot, _):
        for group in range(groups):
            out[group * SPOTS + spot] = rows[
                pl.ds(group * SUBLANES * SPOTS + spot, SUBLANES, stride=SPOTS), :
            ]
        return 0

    lax.fori_loop(0, SPOTS, one, 0, unroll=8)


def conv_rows(src, spread, group, flip, emit):
    for p in range(SIDE):
        sums = [None] * SIDE
        for a in range(TAPS):
            row = p + a - REACH
            if not 0 <= row < SIDE:
                continue
            values = [src[group * SPOTS + row * SIDE + q] for q in range(SIDE)]
            for b in range(TAPS):
                tap = a * TAPS + b
                weight = spread[TAPS * TAPS - 1 - tap if flip else tap]
                for q in range(SIDE):
                    col = q + b - REACH
                    if 0 <= col < SIDE:
                        term = values[col] * weight
                        sums[q] = term if sums[q] is None else sums[q] + term
        for q in range(SIDE):
            emit(p * SIDE + q, sums[q])


def conv_kernel(
    slots, x_ref, taps_ref, _after, _buffer, out_ref, rows, minor, spread, conv
):
    groups = rows.shape[0] // (SUBLANES * SPOTS)
    spread_taps(taps_ref, spread)

    def load(slot, _):
        rows[pl.ds(pl.multiple_of(slot * SPOTS, SPOTS), SPOTS), :] = (
            x_ref[slot].astype(F32).reshape(SPOTS, LANES)
        )
        return 0

    lax.fori_loop(0, slots, load, 0)
    to_patch_minor(rows, minor, groups)

    def convolve(group, _):
        def emit(spot, value):
            conv[pl.ds(group * SUBLANES * SPOTS + spot, SUBLANES, stride=SPOTS), :] = value

        conv_rows(minor, spread, group, False, emit)
        return 0

    lax.fori_loop(0, groups, convolve, 0)
    out_ref[...] = conv[: slots * SPOTS, :]


def shapes_of(x):
    slots, channels = x.shape[0], x.shape[3]
    groups = -(-slots // SUBLANES)
    return slots, channels, slots * SPOTS, groups, groups * SUBLANES * SPOTS


def conv_part(part, x, taps, after, buffer):
    slots, channels, tokens, groups, padded = shapes_of(x)
    base = part * GROUP_STEPS
    anywhere = pl.BlockSpec(memory_space=pl.ANY)
    if buffer is None:
        buffer, aliases = after, {}
    else:
        aliases = {3: 0}
    return pl.pallas_call(
        functools.partial(conv_kernel, slots),
        grid=(GROUP_STEPS,),
        in_specs=[
            pl.BlockSpec((slots, SIDE, SIDE, LANES), lambda j: (0, 0, 0, j + base)),
            pl.BlockSpec((TAPS * TAPS, LANES), lambda j: (0, j + base)),
            anywhere,
            anywhere,
        ],
        out_specs=pl.BlockSpec((tokens, LANES), lambda j: (0, j + base)),
        out_shape=jax.ShapeDtypeStruct((tokens, channels), F32),
        input_output_aliases=aliases,
        scratch_shapes=[
            pltpu.VMEM((padded, LANES), F32),
            pltpu.VMEM((groups * SPOTS, SUBLANES, LANES), F32),
            pltpu.VMEM((TAPS * TAPS, SUBLANES, LANES), F32),
            pltpu.VMEM((padded, LANES), F32),
        ],
        compiler_params=pltpu.CompilerParams(vmem_limit_bytes=SMALL_VMEM),
        cost_estimate=pl.CostEstimate(
            flops=2 * 49 * tokens * LANES * GROUP_STEPS,
            bytes_accessed=6 * tokens * LANES * GROUP_STEPS,
            transcendentals=0,
        ),
        name="conv",
    )(x, taps, after, buffer)


def norm_kernel(
    conv_ref, g_ref, count_ref, gain_ref, shift_ref, scale_ref, _after,
    normed_ref, std_ref, inv_ref, gb_ref,
):
    step = pl.program_id(0)
    count = count_ref[0, 0]
    channels = conv_ref.shape[1]
    parts = [slice(c, c + LANES) for c in range(0, channels, LANES)]
    gain, shift, scale = ([ref[:, c] for c in parts] for ref in (gain_ref, shift_ref, scale_ref))
    tall = 32

    def norm(i, _):
        at = pl.ds(pl.multiple_of(i * tall, tall), tall)
        values = [conv_ref[at, c] for c in parts]
        mean = sum(jnp.sum(v, axis=1, keepdims=True) for v in values) / channels
        values = [v - mean for v in values]
        var = sum(jnp.sum(v * v, axis=1, keepdims=True) for v in values) / channels
        inv = lax.rsqrt(var + 1e-06)
        inv_ref[at, :] = inv
        for c, v in enumerate(values):
            std = v * inv
            std_ref[at, parts[c]] = std
            normed_ref[at, parts[c]] = (std * gain[c] + shift[c]).astype(BF16)
        return 0

    lax.fori_loop(0, NORM_BLOCK // tall, norm, 0, unroll=2)
    for slot in range(NORM_BLOCK // SPOTS):
        live = jnp.where(step * (NORM_BLOCK // SPOTS) + slot < count, 1.0, 0.0)
        for c, lanes in enumerate(parts):
            g = g_ref[slot, :, :, lanes].astype(F32).reshape(SPOTS, LANES)
            gb_ref[slot * SPOTS : (slot + 1) * SPOTS, lanes] = (g * (scale[c] * live)).astype(BF16)


def norm(conv, g, count, gain, shift, scale, after):
    tokens, channels = conv.shape
    block = pl.BlockSpec((NORM_BLOCK, channels), lambda j: (j, 0))
    vector = whole((1, channels))
    return pl.pallas_call(
        norm_kernel,
        grid=(tokens // NORM_BLOCK,),
        in_specs=[
            block,
            pl.BlockSpec((NORM_BLOCK // SPOTS, SIDE, SIDE, channels), lambda j: (j, 0, 0, 0)),
            pl.BlockSpec(memory_space=pltpu.SMEM),
            vector, vector, vector,
            pl.BlockSpec(memory_space=pl.ANY),
        ],
        out_specs=[block, block, pl.BlockSpec((NORM_BLOCK, 1), lambda j: (j, 0)), block],
        out_shape=[
            jax.ShapeDtypeStruct((tokens, channels), BF16),
            jax.ShapeDtypeStruct((tokens, channels), F32),
            jax.ShapeDtypeStruct((tokens, 1), F32),
            jax.ShapeDtypeStruct((tokens, channels), BF16),
        ],
        compiler_params=pltpu.CompilerParams(vmem_limit_bytes=SMALL_VMEM),
        cost_estimate=pl.CostEstimate(
            flops=20 * tokens * channels, bytes_accessed=14 * tokens * channels, transcendentals=0
        ),
        name="norm",
    )(conv, g, count, gain, shift, scale, after)


def tile_of(part, i, across):
    return divmod(part * PART_TILES + i, across)


def aligned(value, to):
    return pl.multiple_of(value * to, to)


def clear(ref):
    tall = 2 * SUBLANES

    def rows(i, _):
        ref[pl.ds(aligned(i, tall), tall), :] = jnp.zeros((tall, ref.shape[1]), F32)
        return 0

    lax.fori_loop(0, ref.shape[0] // tall, rows, 0)


def mlp_kernel(
    count, core_ref, order_ref, mine_ref, theirs_ref, gb_mine_ref, gb_theirs_ref, bias_ref,
    second_ref, *refs,
):
    pieces = refs[:count]
    (
        sums_ref, gn_mine_ref, gn_theirs_ref, grad_bias_ref, scale_ref,
        first, second, sum_first, sum_second, tokens, cots, flipped, grad_normed,
        actives, grads, sems, more_sems,
    ) = refs[count:]
    channels, hidden = first.shape
    half = mine_ref.shape[0]
    chips = second_ref.shape[0]
    cuts = hidden // CUT
    own = pieces[0].shape[0] // (2 * cuts)
    shards = channels // own
    units = hidden // (shards // 2)
    first_rows = shards * PART_TILES * SUBLANES
    part_rows = PART_TILES * 2 * SUBLANES
    tall = 2 * SUBLANES
    dot = functools.partial(lax.dot_general, preferred_element_type=F32)

    loads = [
        pltpu.make_async_copy(src, dst.at[pl.ds(row, half), :], more_sems.at[i])
        for i, (src, dst, row) in enumerate(
            (
                (mine_ref, tokens, 0),
                (theirs_ref, tokens, half),
                (gb_mine_ref, cots, 0),
                (gb_theirs_ref, cots, half),
            )
        )
    ]
    for i, piece in enumerate(pieces):
        for parity in range(2):
            f = order_ref[2 * i + parity]
            for k in range(cuts):
                loads.append(
                    pltpu.make_async_copy(
                        piece.at[pl.ds((parity * cuts + k) * own, own), :],
                        first.at[pl.ds(aligned(f, own), own), pl.ds(k * CUT, CUT)],
                        sems.at[i],
                    )
                )
    for load in loads:
        load.start()

    def unpack_shard(f, _):
        for e in range(chips):
            for i in range(PART_TILES):
                r, c = tile_of(e, i, channels // LANES)
                if r * tall < units:
                    second[
                        pl.ds(pl.multiple_of(f * units + r * tall, tall), tall),
                        c * LANES : (c + 1) * LANES,
                    ] = second_ref[
                        e, pl.ds(pl.multiple_of(f * part_rows + i * tall, tall), tall), :
                    ]
        return 0

    lax.fori_loop(0, shards // 2, unpack_shard, 0)
    clear(grad_normed)
    for load in loads:
        load.wait()

    def flip(j, _):
        at = pl.ds(aligned(j, BLOCK), BLOCK)
        flipped[:, at] = tokens[at, :].T
        return 0

    lax.fori_loop(0, 2 * half // BLOCK, flip, 0)

    def chunk(start, wide):
        units_at = pl.ds(start, wide)

        def block(j, bias_sum):
            at = pl.ds(aligned(j, half), half)
            preact = dot(tokens[at, :], first[:, units_at], (((1,), (0,)), ((), ())))
            preact = preact + bias_ref[:, units_at]
            grad_hidden = dot(cots[at, :], second[units_at, :], (((1,), (1,)), ((), ())))
            prob = 0.5 * (1.0 + lax.erf(preact * 0.7071067811865476))
            actives[at, :wide] = (preact * prob).astype(BF16)
            slope = prob + preact * jnp.exp(-0.5 * preact * preact) * 0.3989422804014327
            grad_preact = (grad_hidden * slope).astype(BF16)
            grads[at, :wide] = grad_preact
            grad_normed[at, :] += dot(grad_preact, first[:, units_at], (((1,), (1,)), ((), ())))
            return bias_sum + jnp.sum(grad_preact.astype(F32), axis=0, keepdims=True)

        grad_bias_ref[:, units_at] = lax.fori_loop(
            0, 2, block, jnp.zeros((1, wide), F32)
        )
        sum_second[units_at, :] = dot(actives[:, :wide], cots[...], (((0,), (0,)), ((), ())))
        sum_first[:, units_at] = dot(flipped[...], grads[:, :wide], (((1,), (0,)), ((), ())))

    def whole_chunk(h, _):
        chunk(aligned(h, BLOCK), BLOCK)
        return 0

    lax.fori_loop(0, hidden // BLOCK, whole_chunk, 0)
    if hidden % BLOCK:
        chunk(hidden // BLOCK * BLOCK, hidden % BLOCK)

    def unload(i, _):
        at = pl.ds(aligned(i, tall), tall)
        gn_mine_ref[at, :] = grad_normed[at, :]
        gn_theirs_ref[at, :] = grad_normed[pl.ds(half + aligned(i, tall), tall), :].astype(BF16)
        return 0

    lax.fori_loop(0, half // tall, unload, 0)

    def scale_rows(i, total):
        at = pl.ds(aligned(i, tall), tall)
        return total + sum_second[at, :] * second[at, :].astype(F32)

    total = lax.fori_loop(0, hidden // tall, scale_rows, jnp.zeros((tall, channels), F32))
    scale_ref[...] = jnp.sum(total, axis=0, keepdims=True)
    none = jnp.zeros((SUBLANES, LANES), F32)

    def pack_pair(pair, _):
        for e in range(chips):
            tiles = []
            for f in range(2):
                for i in range(PART_TILES):
                    r, c = tile_of(e, i, hidden // LANES)
                    row = pl.multiple_of((2 * pair + f) * own + r * SUBLANES, SUBLANES)
                    tiles.append(
                        sum_first[pl.ds(row, SUBLANES), c * LANES : (c + 1) * LANES]
                        if r * SUBLANES < own
                        else none
                    )
            for i in range(0, len(tiles), 2):
                at = pl.multiple_of(pair * part_rows + i * SUBLANES, tall)
                sums_ref[e, pl.ds(at, tall), :] = jnp.concatenate(tiles[i : i + 2]).astype(BF16)
        return 0

    lax.fori_loop(0, shards // 2, pack_pair, 0)

    def pack_shard(f, _):
        for e in range(chips):
            for i in range(PART_TILES):
                r, c = tile_of(e, i, channels // LANES)
                at = pl.multiple_of(first_rows + f * part_rows + i * tall, tall)
                if r * tall < units:
                    row = pl.multiple_of(f * units + r * tall, tall)
                    value = sum_second[pl.ds(row, tall), c * LANES : (c + 1) * LANES]
                else:
                    value = jnp.zeros((tall, LANES), F32)
                sums_ref[e, pl.ds(at, tall), :] = value.astype(BF16)
        return 0

    lax.fori_loop(0, shards // 2, pack_shard, 0)


def mlp(core, order, mine, theirs, gb_mine, gb_theirs, bias, second, pieces):
    tokens, channels = mine.shape
    count, hidden = len(pieces), bias.shape[1]
    sums = (second.shape[0], 2 * count * PART_TILES * SUBLANES + second.shape[1], LANES)
    smem = pl.BlockSpec(memory_space=pltpu.SMEM)
    vmem = pl.BlockSpec(memory_space=pltpu.VMEM)
    anywhere = pl.BlockSpec(memory_space=pl.ANY)
    return pl.pallas_call(
        functools.partial(mlp_kernel, count),
        in_specs=[smem, smem] + [anywhere] * 4 + [vmem, vmem] + [anywhere] * count,
        out_specs=[vmem] * 5,
        out_shape=[
            jax.ShapeDtypeStruct(sums, BF16),
            jax.ShapeDtypeStruct((tokens, channels), F32),
            jax.ShapeDtypeStruct((tokens, channels), BF16),
            jax.ShapeDtypeStruct((1, hidden), F32),
            jax.ShapeDtypeStruct((1, channels), F32),
        ],
        scratch_shapes=[
            pltpu.VMEM((channels, hidden), BF16),
            pltpu.VMEM((hidden, channels), BF16),
            pltpu.VMEM((channels, hidden), F32),
            pltpu.VMEM((hidden, channels), F32),
            pltpu.VMEM((2 * tokens, channels), BF16),
            pltpu.VMEM((2 * tokens, channels), BF16),
            pltpu.VMEM((channels, 2 * tokens), BF16),
            pltpu.VMEM((2 * tokens, channels), F32),
            pltpu.VMEM((2 * tokens, BLOCK), BF16),
            pltpu.VMEM((2 * tokens, BLOCK), BF16),
            pltpu.SemaphoreType.DMA((count,)),
            pltpu.SemaphoreType.DMA((4,)),
        ],
        compiler_params=pltpu.CompilerParams(vmem_limit_bytes=VMEM_LIMIT),
        cost_estimate=pl.CostEstimate(
            flops=20 * tokens * channels * hidden,
            bytes_accessed=12 * hidden * channels,
            transcendentals=4 * tokens * hidden,
        ),
        name="mlp",
    )(core, order, mine, theirs, gb_mine, gb_theirs, bias, second, *pieces)


def unnorm_kernel(gn_ref, gn_other_ref, std_ref, inv_ref, gain_ref, grad_conv_ref, channel_ref):
    step = pl.program_id(0)
    channels = gn_ref.shape[1]
    parts = [slice(c, c + LANES) for c in range(0, channels, LANES)]
    gain = [gain_ref[:, c] for c in parts]
    tall = 32

    @pl.when(step == 0)
    def _():
        channel_ref[...] = jnp.zeros_like(channel_ref)

    def one(i, sums):
        at = pl.ds(pl.multiple_of(i * tall, tall), tall)
        inv = inv_ref[at, :]
        scaled, new = [], []
        for c, lanes in enumerate(parts):
            gn = gn_ref[at, lanes] + gn_other_ref[at, lanes].astype(F32)
            std = std_ref[at, lanes]
            product = gn * std
            gain_sum, shift_sum = sums[2 * c], sums[2 * c + 1]
            for r in range(0, tall, SUBLANES):
                gain_sum = gain_sum + product[r : r + SUBLANES]
                shift_sum = shift_sum + gn[r : r + SUBLANES]
            new += [gain_sum, shift_sum]
            scaled.append((gn * gain[c], product * gain[c], std))
        mean = sum(jnp.sum(v[0], axis=1, keepdims=True) for v in scaled) / channels
        mean_std = sum(jnp.sum(v[1], axis=1, keepdims=True) for v in scaled) / channels
        for c, (v, _, std) in enumerate(scaled):
            grad_conv_ref[at, parts[c]] = inv * (v - mean - std * mean_std)
        return tuple(new)

    zero = jnp.zeros((SUBLANES, LANES), F32)
    sums = lax.fori_loop(0, NORM_BLOCK // tall, one, (zero,) * (2 * len(parts)))
    for c, lanes in enumerate(parts):
        channel_ref[0:1, lanes] += jnp.sum(sums[2 * c], axis=0, keepdims=True)
        channel_ref[1:2, lanes] += jnp.sum(sums[2 * c + 1], axis=0, keepdims=True)


def unnorm(gn, gn_other, std, inv, gain):
    tokens, channels = gn.shape
    block = pl.BlockSpec((NORM_BLOCK, channels), lambda j: (j, 0))
    return pl.pallas_call(
        unnorm_kernel,
        grid=(tokens // NORM_BLOCK,),
        in_specs=[
            block, block, block,
            pl.BlockSpec((NORM_BLOCK, 1), lambda j: (j, 0)),
            whole((1, channels)),
        ],
        out_specs=[block, whole((2, channels))],
        out_shape=[
            jax.ShapeDtypeStruct((tokens, channels), F32),
            jax.ShapeDtypeStruct((2, channels), F32),
        ],
        compiler_params=pltpu.CompilerParams(vmem_limit_bytes=SMALL_VMEM),
        cost_estimate=pl.CostEstimate(
            flops=20 * tokens * channels, bytes_accessed=14 * tokens * channels, transcendentals=0
        ),
        name="unnorm",
    )(gn, gn_other, std, inv, gain)


def load_grads(grad_ref, rows, grad_minor, groups, tokens):
    rows[:tokens, :] = grad_ref[...]
    if rows.shape[0] > tokens:
        rows[tokens:, :] = jnp.zeros((rows.shape[0] - tokens, LANES), F32)
    to_patch_minor(rows, grad_minor, groups)


def taps_kernel(
    slots, x_ref, grad_ref, _after, _buffer, grad_taps_ref, rows, minor, grad_minor, tap_sums
):
    groups = rows.shape[0] // (SUBLANES * SPOTS)
    load_grads(grad_ref, rows, grad_minor, groups, slots * SPOTS)

    def load(slot, _):
        rows[pl.ds(pl.multiple_of(slot * SPOTS, SPOTS), SPOTS), :] = (
            x_ref[slot].astype(F32).reshape(SPOTS, LANES)
        )
        return 0

    lax.fori_loop(0, slots, load, 0)
    to_patch_minor(rows, minor, groups)

    def taps(group, _):
        for a in range(TAPS):
            sums = [jnp.where(group == 0, 0.0, tap_sums[a * TAPS + b]) for b in range(TAPS)]
            for p in range(SIDE):
                row = p + a - REACH
                if not 0 <= row < SIDE:
                    continue
                values = [minor[group * SPOTS + row * SIDE + q] for q in range(SIDE)]
                grads = [grad_minor[group * SPOTS + p * SIDE + q] for q in range(SIDE)]
                for b in range(TAPS):
                    for q in range(SIDE):
                        col = q + b - REACH
                        if 0 <= col < SIDE:
                            sums[b] = sums[b] + grads[q] * values[col]
            for b in range(TAPS):
                tap_sums[a * TAPS + b] = sums[b]
        return 0

    lax.fori_loop(0, groups, taps, 0)
    for tap in range(TAPS * TAPS):
        grad_taps_ref[tap : tap + 1, :] = jnp.sum(tap_sums[tap], axis=0, keepdims=True)


def taps_part(part, x, grad_conv, after, buffer):
    slots, channels, tokens, groups, padded = shapes_of(x)
    base = part * GROUP_STEPS
    anywhere = pl.BlockSpec(memory_space=pl.ANY)
    if buffer is None:
        buffer, aliases = after, {}
    else:
        aliases = {3: 0}
    return pl.pallas_call(
        functools.partial(taps_kernel, slots),
        grid=(GROUP_STEPS,),
        in_specs=[
            pl.BlockSpec((slots, SIDE, SIDE, LANES), lambda j: (0, 0, 0, j + base)),
            pl.BlockSpec((tokens, LANES), lambda j: (0, j + base)),
            anywhere,
            anywhere,
        ],
        out_specs=pl.BlockSpec((TAPS * TAPS, LANES), lambda j: (0, j + base)),
        out_shape=jax.ShapeDtypeStruct((TAPS * TAPS, channels), F32),
        input_output_aliases=aliases,
        scratch_shapes=[
            pltpu.VMEM((padded, LANES), F32),
            pltpu.VMEM((groups * SPOTS, SUBLANES, LANES), F32),
            pltpu.VMEM((groups * SPOTS, SUBLANES, LANES), F32),
            pltpu.VMEM((TAPS * TAPS, SUBLANES, LANES), F32),
        ],
        compiler_params=pltpu.CompilerParams(vmem_limit_bytes=SMALL_VMEM),
        cost_estimate=pl.CostEstimate(
            flops=2 * 49 * tokens * LANES * GROUP_STEPS,
            bytes_accessed=6 * tokens * LANES * GROUP_STEPS,
            transcendentals=0,
        ),
        name="taps",
    )(x, grad_conv, after, buffer)


def back_kernel(
    slots, g_ref, grad_ref, count_ref, taps_ref, _after, _buffer, in_grad_ref,
    rows, grad_minor, spread, result,
):
    groups = rows.shape[0] // (SUBLANES * SPOTS)
    spread_taps(taps_ref, spread)
    load_grads(grad_ref, rows, grad_minor, groups, slots * SPOTS)

    def convolve(group, _):
        def emit(spot, value):
            result[pl.ds(group * SUBLANES * SPOTS + spot, SUBLANES, stride=SPOTS), :] = value

        conv_rows(grad_minor, spread, group, True, emit)
        return 0

    lax.fori_loop(0, groups, convolve, 0)
    count = count_ref[0, 0]

    def finish(slot, _):
        live = jnp.where(slot < count, 1.0, 0.0)
        g = g_ref[slot].astype(F32) * live
        at = pl.ds(pl.multiple_of(slot * SPOTS, SPOTS), SPOTS)
        in_grad_ref[slot] = g + result[at, :].reshape(SIDE, SIDE, LANES)
        return 0

    lax.fori_loop(0, slots, finish, 0)


def back_part(part, g, grad_conv, count, taps, after, buffer):
    slots, channels, tokens, groups, padded = shapes_of(g)
    base = part * GROUP_STEPS
    anywhere = pl.BlockSpec(memory_space=pl.ANY)
    if buffer is None:
        buffer, aliases = after, {}
    else:
        aliases = {5: 0}
    return pl.pallas_call(
        functools.partial(back_kernel, slots),
        grid=(GROUP_STEPS,),
        in_specs=[
            pl.BlockSpec((slots, SIDE, SIDE, LANES), lambda j: (0, 0, 0, j + base)),
            pl.BlockSpec((tokens, LANES), lambda j: (0, j + base)),
            pl.BlockSpec(memory_space=pltpu.SMEM),
            pl.BlockSpec((TAPS * TAPS, LANES), lambda j: (0, j + base)),
            anywhere,
            anywhere,
        ],
        out_specs=pl.BlockSpec((slots, SIDE, SIDE, LANES), lambda j: (0, 0, 0, j + base)),
        out_shape=jax.ShapeDtypeStruct((slots, SIDE, SIDE, channels), F32),
        input_output_aliases=aliases,
        scratch_shapes=[
            pltpu.VMEM((padded, LANES), F32),
            pltpu.VMEM((groups * SPOTS, SUBLANES, LANES), F32),
            pltpu.VMEM((TAPS * TAPS, SUBLANES, LANES), F32),
            pltpu.VMEM((padded, LANES), F32),
        ],
        compiler_params=pltpu.CompilerParams(vmem_limit_bytes=SMALL_VMEM),
        cost_estimate=pl.CostEstimate(
            flops=2 * 49 * tokens * LANES * GROUP_STEPS,
            bytes_accessed=10 * tokens * LANES * GROUP_STEPS,
            transcendentals=0,
        ),
        name="back",
    )(g, grad_conv, count, taps, after, buffer)


def device_index(x, y, z, core):
    high, low = divmod(y % Y, 2)
    return ((x % X) * 4 + high * 2 + core) * (2 * Z) + (z % Z) * 2 + low


def move(value, dy=0, dz=0, flip=0):
    pairs = [
        (device_index(x, y, z, core), device_index(x, y + dy, z + dz, core ^ flip))
        for x in range(X)
        for y in range(Y)
        for z in range(Z)
        for core in range(2)
    ]
    return lax.ppermute(value, AXES, pairs)


def gather_pieces(piece, z, low, between):
    other = lax.ppermute(piece, "fsdp", [(i, i ^ 1) for i in range(2 * Z)])
    pair = jnp.concatenate([piece, other])
    right, left = move(pair, dz=1), move(pair, dz=-1)
    right, left, made = between(right, left)
    pieces, away = [pair, right, left], [0, Z - 1, 1]
    for step in range(2, Z // 2 + 1):
        right = move(right, dz=1)
        pieces.append(right)
        away.append(Z - step)
        if step < Z // 2:
            left = move(left, dz=-1)
            pieces.append(left)
            away.append(step)
    order = [(z + s) % Z * 2 + (low ^ parity) for s in away for parity in range(2)]
    return jnp.stack(order).astype(jnp.int32), pieces, made


def copies_kernel(kept_ref, swapped_ref, _right, _left, out_ref, _right_out, _left_out):
    def shard(f, _):
        both = [kept_ref[f].astype(F32), swapped_ref[f].astype(F32)]
        both = jnp.concatenate(both).astype(BF16)
        rows = both.shape[0]
        for e in range(out_ref.shape[0]):
            out_ref[e, pl.ds(pl.multiple_of(f * rows, rows), rows), :] = both
        return 0

    lax.fori_loop(0, kept_ref.shape[0], shard, 0)


def copies(chips, kept, swapped, right, left):
    shards, rows, lanes = kept.shape
    vmem = pl.BlockSpec(memory_space=pltpu.VMEM)
    anywhere = pl.BlockSpec(memory_space=pl.ANY)
    return pl.pallas_call(
        copies_kernel,
        in_specs=[vmem, vmem, anywhere, anywhere],
        out_specs=[vmem, anywhere, anywhere],
        out_shape=[
            jax.ShapeDtypeStruct((chips, shards * 2 * rows, lanes), BF16),
            jax.ShapeDtypeStruct(right.shape, BF16),
            jax.ShapeDtypeStruct(left.shape, BF16),
        ],
        input_output_aliases={2: 1, 3: 2},
        compiler_params=pltpu.CompilerParams(vmem_limit_bytes=SMALL_VMEM),
        name="copies",
    )(kept, swapped, right, left)


def add_up_kernel(terms_ref, _after, out_ref):
    tall = 8 * SUBLANES

    def rows(i, _):
        at = pl.ds(pl.multiple_of(i * tall, tall), tall)
        total = terms_ref[0, at, :].astype(F32)
        for e in range(1, terms_ref.shape[0]):
            total = total + terms_ref[e, at, :].astype(F32)
        out_ref[at, :] = total.astype(BF16)
        return 0

    lax.fori_loop(0, terms_ref.shape[1] // tall, rows, 0, unroll=2)


def add_up(terms, after):
    return pl.pallas_call(
        add_up_kernel,
        in_specs=[
            pl.BlockSpec(memory_space=pltpu.VMEM),
            pl.BlockSpec(memory_space=pl.ANY),
        ],
        out_shape=jax.ShapeDtypeStruct(terms.shape[1:], BF16),
        compiler_params=pltpu.CompilerParams(vmem_limit_bytes=SMALL_VMEM),
        name="add_up",
    )(terms, after)


def finish_kernel(factor, side_ref, terms_ref, first_ref, second_ref, small_ref):
    side = side_ref[0]
    chips = terms_ref.shape[0] // 2
    small_rows = PART_TILES * 2 * SUBLANES
    half = small_rows // 2
    wide = first_ref.shape[1] // 2 // LANES
    small = None
    for e in range(chips):
        for core in range(2):
            part = terms_ref[2 * e + core, :small_rows, :].astype(F32) * factor
            for i in range(PART_TILES):
                r, c = tile_of(e, i, wide)
                if r * SUBLANES < first_ref.shape[0]:
                    lane = (core * wide + c) * LANES
                    first_ref[r * SUBLANES : (r + 1) * SUBLANES, lane : lane + LANES] = part[
                        i * SUBLANES : (i + 1) * SUBLANES
                    ]
            more = terms_ref[2 * e + core, small_rows:, :].astype(F32)
            small = more if small is None else small + more
        part = jnp.concatenate(
            [
                terms_ref[2 * e + core, :small_rows, :].astype(F32)[half:]
                for core in (side, 1 - side)
            ]
        )
        part = part * factor
        for i in range(PART_TILES):
            r, c = tile_of(e, i, second_ref.shape[1] // LANES)
            if r * 2 * SUBLANES < second_ref.shape[0]:
                second_ref[r * 2 * SUBLANES : (r + 1) * 2 * SUBLANES, c * LANES : (c + 1) * LANES] = (
                    part[i * 2 * SUBLANES : (i + 1) * 2 * SUBLANES]
                )
    small_ref[...] = small * factor


def finish(side, terms, first_shape, second_shape, factor):
    small = (terms.shape[1] - PART_TILES * 2 * SUBLANES, LANES)
    return pl.pallas_call(
        functools.partial(finish_kernel, factor),
        in_specs=[
            pl.BlockSpec(memory_space=pltpu.SMEM),
            pl.BlockSpec(memory_space=pltpu.VMEM),
        ],
        out_shape=[
            jax.ShapeDtypeStruct(first_shape, F32),
            jax.ShapeDtypeStruct(second_shape, F32),
            jax.ShapeDtypeStruct(small, F32),
        ],
        compiler_params=pltpu.CompilerParams(vmem_limit_bytes=SMALL_VMEM),
        name="finish",
    )(side, terms)


def pack(rows):
    count, width = rows.shape[-2:]
    half = -(-count // 2)
    lead = [(0, 0)] * (rows.ndim - 2)
    rows = jnp.pad(rows, lead + [(0, 2 * half - count), (0, 0)])
    rows = jnp.concatenate([rows[..., :half, :], rows[..., half:, :]], axis=-1)
    return jnp.pad(rows, lead + [(0, -half % (2 * SUBLANES)), (0, LANES - 2 * width)])


def unpack(packed, count, width):
    half = -(-count // 2)
    rows = [packed[..., :half, :width], packed[..., :half, width : 2 * width]]
    return jnp.concatenate(rows, axis=-2)[..., :count, :]


def local(
    patches,
    out_grad,
    row_counts,
    dw_kernel,
    ln_gain,
    ln_bias,
    w_first,
    first_bias,
    w_second,
    layer_scale,
):
    fsdp, dp = lax.axis_size("fsdp"), lax.axis_size("dp")
    own = ln_gain.shape[0]
    units = first_bias.shape[0]
    channels, hidden = own * fsdp, units * fsdp
    mine = hidden // 2
    tap_count = dw_kernel.shape[0]
    dp_index, fsdp_index = lax.axis_index("dp"), lax.axis_index("fsdp")
    core = dp_index % 2
    z, low = fsdp_index // 2, fsdp_index % 2

    chip, chips = dp_index // 2, dp // 2
    side = fsdp_index // (fsdp // 2)
    same_core = [[2 * i + c for i in range(chips)] for c in range(2)]
    flat = (PART_TILES * SUBLANES, LANES)

    tall, across = units // (2 * SUBLANES), channels // LANES
    tiles = w_second.reshape(tall, 2 * SUBLANES, across, LANES).transpose(0, 2, 1, 3)
    tiles = tiles.reshape(tall * across, 2 * SUBLANES, LANES)
    tiles = jnp.pad(tiles, ((0, chips * PART_TILES - tall * across), (0, 0), (0, 0)))
    tiles = tiles.reshape(chips * 2, *flat)
    tiles = lax.dynamic_index_in_dim(tiles, 2 * chip + (core ^ side), 0, keepdims=False)
    vectors = [ln_gain[None], ln_bias[None], layer_scale[None], first_bias.reshape(-1, own)]
    small = jnp.concatenate([dw_kernel] + vectors)
    lines = small.shape[0]
    small = jnp.concatenate([tiles, pack(small)])
    small = lax.all_to_all(
        jnp.broadcast_to(small, (fsdp,) + small.shape), "fsdp", 0, 0, tiled=True
    )
    tiles, small = small[:, : flat[0]], unpack(small[:, flat[0] :], lines, own)
    kept = lax.dynamic_slice_in_dim(tiles, core * (fsdp // 2), fsdp // 2)
    swapped = move(lax.dynamic_slice_in_dim(tiles, (1 - core) * (fsdp // 2), fsdp // 2), flip=1)

    def between(right, left):
        made, right, left = copies(chips, kept, swapped, right, left)
        made = lax.all_to_all(made, "dp", 0, 0, tiled=True, axis_index_groups=same_core)
        return right, left, made

    part = lax.dynamic_slice_in_dim(w_first, core * mine, mine, 1)
    part = [part[:, k * CUT : (k + 1) * CUT] for k in range(mine // CUT)]
    order, pieces, second = gather_pieces(jnp.concatenate(part), z, low, between)

    taps = small[:, :tap_count].transpose(1, 0, 2).reshape(tap_count, channels).astype(F32)
    gain, shift, scale = (
        small[:, tap_count + i].reshape(1, channels).astype(F32) for i in range(3)
    )
    bias = small[:, tap_count + 3 :].reshape(1, hidden).astype(F32)
    bias = lax.dynamic_slice_in_dim(bias, core * mine, mine, 1)

    x, g = patches[0], out_grad[0]
    conv = conv_part(0, x, taps, pieces[1], None)
    conv = conv_part(1, x, taps, pieces[4], conv)
    conv = conv_part(2, x, taps, pieces[6], conv)
    normed, std, inv, gb = norm(conv, g, row_counts, gain, shift, scale, pieces[7])
    normed_other, gb_other = move(normed, flip=1), move(gb, flip=1)
    terms, gn_mine, gn_theirs, grad_bias, scale_sum = mlp(
        core.reshape(1), order, normed, normed_other, gb, gb_other, bias, second, pieces
    )
    gn_other = move(gn_theirs, flip=1)
    scale_sum = scale_sum / scale
    grad_conv, channel_sums = unnorm(gn_mine, gn_other, std, inv, gain)
    grad_taps = taps_part(0, x, grad_conv, terms, None)
    grad_taps = taps_part(1, x, grad_conv, terms, grad_taps)
    grad_taps = taps_part(2, x, grad_conv, terms, grad_taps)
    in_grad = back_part(0, g, grad_conv, row_counts, taps, terms, None)
    in_grad = back_part(1, g, grad_conv, row_counts, taps, terms, in_grad)
    in_grad = back_part(2, g, grad_conv, row_counts, taps, terms, in_grad)

    terms = lax.all_to_all(terms, "dp", 0, 0, tiled=True, axis_index_groups=same_core)
    terms = add_up(terms, in_grad)
    first = terms[: fsdp * flat[0]].reshape((fsdp,) + flat)
    second = terms[fsdp * flat[0] :].reshape((fsdp // 2, 2) + flat)
    swapped = move(second[:, 1], flip=1)
    second = jnp.where(
        core == 0,
        jnp.concatenate([second[:, 0], swapped]),
        jnp.concatenate([swapped, second[:, 0]]),
    )
    sums = jnp.concatenate([grad_taps, channel_sums, scale_sum], axis=0)
    sums = sums.reshape(sums.shape[0], fsdp, own).transpose(1, 0, 2)
    grad_bias = jnp.concatenate([grad_bias, grad_bias], axis=1).reshape(fsdp, -1, own)
    computed = (jnp.arange(fsdp, dtype=jnp.int32) // (fsdp // 2) == core)[:, None, None]
    sums = jnp.concatenate([sums, jnp.where(computed, grad_bias, 0.0)], axis=1)
    terms = jnp.concatenate([first, second, pack(sums.astype(BF16))], axis=1)
    terms = lax.all_to_all(terms, "fsdp", 0, 0, tiled=True)
    terms = jnp.sum(terms.astype(F32), axis=0).astype(BF16)
    terms = lax.all_to_all(
        jnp.broadcast_to(terms[None], (dp,) + terms.shape), "dp", 0, 0, tiled=True
    )
    factor = 1.0 / math.sqrt(fsdp * dp * ROWS * SPOTS)
    first, second, sums = finish(
        side.reshape(1), terms, (own, hidden), (units, channels), factor
    )
    sums = unpack(sums, lines, own)
    return (
        in_grad[None],
        first,
        second,
        sums[:tap_count],
        sums[tap_count + 3 :].reshape(units),
        sums[tap_count : tap_count + 3],
    )


def solution(mesh):
    placed = (
        P("fsdp", "dp", None, None, None),
        P("fsdp", "dp", None, None, None),
        P("fsdp", "dp"),
        P(None, "fsdp"),
        P("fsdp"),
        P("fsdp"),
        P("fsdp", None),
        P("fsdp"),
        P("fsdp", None),
        P("fsdp"),
    )
    return jax.shard_map(
        local,
        mesh=mesh,
        in_specs=placed,
        out_specs=(
            P("fsdp", "dp", None, None, None),
            P("fsdp", None),
            P("fsdp", None),
            P(None, "fsdp"),
            P("fsdp"),
            P(None, "fsdp"),
        ),
        check_vma=False,
    )
```

```python
import functools
import math

import jax
import jax.numpy as jnp
from jax import lax
from jax.experimental import pallas as pl
from jax.experimental.pallas import tpu as pltpu
from jax.sharding import PartitionSpec as P

ROWS = 8
LANES = 128
SUBLANES = 8
SIDE = 8
SPOTS = SIDE * SIDE
REACH = 3
TAPS = 7
BLOCK = 256
NORM_BLOCK = 128
PART_TILES = 7
GROUP_STEPS = 2
CUT = 384
AXES = ("dp", "fsdp")
X, Y, Z = 4, 4, 8
BF16, F32 = jnp.bfloat16, jnp.float32
VMEM_LIMIT = 56 * 1024 * 1024
SMALL_VMEM = 24 * 1024 * 1024


def whole(shape):
    return pl.BlockSpec(shape, lambda *_: (0,) * len(shape))


def spread_taps(taps_ref, spread):
    for tap in range(TAPS * TAPS):
        spread[tap] = jnp.broadcast_to(taps_ref[tap : tap + 1, :], (SUBLANES, LANES))


def to_patch_minor(rows, out, groups):
    def one(spot, _):
        for group in range(groups):
            out[group * SPOTS + spot] = rows[
                pl.ds(group * SUBLANES * SPOTS + spot, SUBLANES, stride=SPOTS), :
            ]
        return 0

    lax.fori_loop(0, SPOTS, one, 0, unroll=8)


def conv_rows(src, spread, group, flip, emit):
    for p in range(SIDE):
        sums = [None] * SIDE
        for a in range(TAPS):
            row = p + a - REACH
            if not 0 <= row < SIDE:
                continue
            values = [src[group * SPOTS + row * SIDE + q] for q in range(SIDE)]
            for b in range(TAPS):
                tap = a * TAPS + b
                weight = spread[TAPS * TAPS - 1 - tap if flip else tap]
                for q in range(SIDE):
                    col = q + b - REACH
                    if 0 <= col < SIDE:
                        term = values[col] * weight
                        sums[q] = term if sums[q] is None else sums[q] + term
        for q in range(SIDE):
            emit(p * SIDE + q, sums[q])


def conv_kernel(
    slots, x_ref, taps_ref, _after, _buffer, out_ref, rows, minor, spread, conv
):
    groups = rows.shape[0] // (SUBLANES * SPOTS)
    spread_taps(taps_ref, spread)

    def load(slot, _):
        rows[pl.ds(pl.multiple_of(slot * SPOTS, SPOTS), SPOTS), :] = (
            x_ref[slot].astype(F32).reshape(SPOTS, LANES)
        )
        return 0

    lax.fori_loop(0, slots, load, 0)
    to_patch_minor(rows, minor, groups)

    def convolve(group, _):
        def emit(spot, value):
            conv[pl.ds(group * SUBLANES * SPOTS + spot, SUBLANES, stride=SPOTS), :] = value

        conv_rows(minor, spread, group, False, emit)
        return 0

    lax.fori_loop(0, groups, convolve, 0)
    out_ref[...] = conv[: slots * SPOTS, :]


def shapes_of(x):
    slots, channels = x.shape[0], x.shape[3]
    groups = -(-slots // SUBLANES)
    return slots, channels, slots * SPOTS, groups, groups * SUBLANES * SPOTS


def conv_part(part, x, taps, after, buffer):
    slots, channels, tokens, groups, padded = shapes_of(x)
    base = part * GROUP_STEPS
    anywhere = pl.BlockSpec(memory_space=pl.ANY)
    if buffer is None:
        buffer, aliases = after, {}
    else:
        aliases = {3: 0}
    return pl.pallas_call(
        functools.partial(conv_kernel, slots),
        grid=(GROUP_STEPS,),
        in_specs=[
            pl.BlockSpec((slots, SIDE, SIDE, LANES), lambda j: (0, 0, 0, j + base)),
            pl.BlockSpec((TAPS * TAPS, LANES), lambda j: (0, j + base)),
            anywhere,
            anywhere,
        ],
        out_specs=pl.BlockSpec((tokens, LANES), lambda j: (0, j + base)),
        out_shape=jax.ShapeDtypeStruct((tokens, channels), F32),
        input_output_aliases=aliases,
        scratch_shapes=[
            pltpu.VMEM((padded, LANES), F32),
            pltpu.VMEM((groups * SPOTS, SUBLANES, LANES), F32),
            pltpu.VMEM((TAPS * TAPS, SUBLANES, LANES), F32),
            pltpu.VMEM((padded, LANES), F32),
        ],
        compiler_params=pltpu.CompilerParams(vmem_limit_bytes=SMALL_VMEM),
        cost_estimate=pl.CostEstimate(
            flops=2 * 49 * tokens * LANES * GROUP_STEPS,
            bytes_accessed=6 * tokens * LANES * GROUP_STEPS,
            transcendentals=0,
        ),
        name="conv",
    )(x, taps, after, buffer)


def norm_kernel(
    conv_ref, g_ref, count_ref, gain_ref, shift_ref, scale_ref, _after,
    normed_ref, std_ref, inv_ref, gb_ref,
):
    step = pl.program_id(0)
    count = count_ref[0, 0]
    channels = conv_ref.shape[1]
    parts = [slice(c, c + LANES) for c in range(0, channels, LANES)]
    gain, shift, scale = ([ref[:, c] for c in parts] for ref in (gain_ref, shift_ref, scale_ref))
    tall = 32

    def norm(i, _):
        at = pl.ds(pl.multiple_of(i * tall, tall), tall)
        values = [conv_ref[at, c] for c in parts]
        mean = sum(jnp.sum(v, axis=1, keepdims=True) for v in values) / channels
        values = [v - mean for v in values]
        var = sum(jnp.sum(v * v, axis=1, keepdims=True) for v in values) / channels
        inv = lax.rsqrt(var + 1e-06)
        inv_ref[at, :] = inv
        for c, v in enumerate(values):
            std = v * inv
            std_ref[at, parts[c]] = std
            normed_ref[at, parts[c]] = (std * gain[c] + shift[c]).astype(BF16)
        return 0

    lax.fori_loop(0, NORM_BLOCK // tall, norm, 0, unroll=2)
    for slot in range(NORM_BLOCK // SPOTS):
        live = jnp.where(step * (NORM_BLOCK // SPOTS) + slot < count, 1.0, 0.0)
        for c, lanes in enumerate(parts):
            g = g_ref[slot, :, :, lanes].astype(F32).reshape(SPOTS, LANES)
            gb_ref[slot * SPOTS : (slot + 1) * SPOTS, lanes] = (g * (scale[c] * live)).astype(BF16)


def norm(conv, g, count, gain, shift, scale, after):
    tokens, channels = conv.shape
    block = pl.BlockSpec((NORM_BLOCK, channels), lambda j: (j, 0))
    vector = whole((1, channels))
    return pl.pallas_call(
        norm_kernel,
        grid=(tokens // NORM_BLOCK,),
        in_specs=[
            block,
            pl.BlockSpec((NORM_BLOCK // SPOTS, SIDE, SIDE, channels), lambda j: (j, 0, 0, 0)),
            pl.BlockSpec(memory_space=pltpu.SMEM),
            vector, vector, vector,
            pl.BlockSpec(memory_space=pl.ANY),
        ],
        out_specs=[block, block, pl.BlockSpec((NORM_BLOCK, 1), lambda j: (j, 0)), block],
        out_shape=[
            jax.ShapeDtypeStruct((tokens, channels), BF16),
            jax.ShapeDtypeStruct((tokens, channels), F32),
            jax.ShapeDtypeStruct((tokens, 1), F32),
            jax.ShapeDtypeStruct((tokens, channels), BF16),
        ],
        compiler_params=pltpu.CompilerParams(vmem_limit_bytes=SMALL_VMEM),
        cost_estimate=pl.CostEstimate(
            flops=20 * tokens * channels, bytes_accessed=14 * tokens * channels, transcendentals=0
        ),
        name="norm",
    )(conv, g, count, gain, shift, scale, after)


def tile_of(part, i, across):
    return divmod(part * PART_TILES + i, across)


def aligned(value, to):
    return pl.multiple_of(value * to, to)


def clear(ref):
    tall = 2 * SUBLANES

    def rows(i, _):
        ref[pl.ds(aligned(i, tall), tall), :] = jnp.zeros((tall, ref.shape[1]), F32)
        return 0

    lax.fori_loop(0, ref.shape[0] // tall, rows, 0)


def mlp_kernel(
    count, core_ref, order_ref, mine_ref, theirs_ref, gb_mine_ref, gb_theirs_ref, bias_ref,
    second_ref, *refs,
):
    pieces = refs[:count]
    (
        sums_out, gn_mine_out, gn_theirs_out, grad_bias_ref, scale_ref,
        first, second, sum_first, sum_second, tokens, cots, flipped, grad_normed,
        actives, grads, sums_ref, gn_theirs_ref, sems, more_sems, out_sems,
    ) = refs[count:]
    channels, hidden = first.shape
    half = mine_ref.shape[0]
    chips = second_ref.shape[0]
    cuts = hidden // CUT
    own = pieces[0].shape[0] // (2 * cuts)
    shards = channels // own
    units = hidden // (shards // 2)
    first_rows = shards * PART_TILES * SUBLANES
    part_rows = PART_TILES * 2 * SUBLANES
    tall = 2 * SUBLANES
    dot = functools.partial(lax.dot_general, preferred_element_type=F32)

    loads = [
        pltpu.make_async_copy(src, dst.at[pl.ds(row, half), :], more_sems.at[i])
        for i, (src, dst, row) in enumerate(
            (
                (mine_ref, tokens, 0),
                (theirs_ref, tokens, half),
                (gb_mine_ref, cots, 0),
                (gb_theirs_ref, cots, half),
            )
        )
    ]
    for i, piece in enumerate(pieces):
        for parity in range(2):
            f = order_ref[2 * i + parity]
            for k in range(cuts):
                loads.append(
                    pltpu.make_async_copy(
                        piece.at[pl.ds((parity * cuts + k) * own, own), :],
                        first.at[pl.ds(aligned(f, own), own), pl.ds(k * CUT, CUT)],
                        sems.at[i],
                    )
                )
    for load in loads:
        load.start()

    def unpack_shard(f, _):
        for e in range(chips):
            for i in range(PART_TILES):
                r, c = tile_of(e, i, channels // LANES)
                if r * tall < units:
                    second[
                        pl.ds(pl.multiple_of(f * units + r * tall, tall), tall),
                        c * LANES : (c + 1) * LANES,
                    ] = second_ref[
                        e, pl.ds(pl.multiple_of(f * part_rows + i * tall, tall), tall), :
                    ]
        return 0

    lax.fori_loop(0, shards // 2, unpack_shard, 0)
    clear(grad_normed)
    for load in loads:
        load.wait()

    def flip(j, _):
        at = pl.ds(aligned(j, BLOCK), BLOCK)
        flipped[:, at] = tokens[at, :].T
        return 0

    lax.fori_loop(0, 2 * half // BLOCK, flip, 0)

    def chunk(start, wide, slot):
        units_at = pl.ds(start, wide)
        lanes = pl.ds(slot * BLOCK, wide)

        def block(j, bias_sum):
            at = pl.ds(aligned(j, half), half)
            preact = dot(tokens[at, :], first[:, units_at], (((1,), (0,)), ((), ())))
            preact = preact + bias_ref[:, units_at]
            grad_hidden = dot(cots[at, :], second[units_at, :], (((1,), (1,)), ((), ())))
            prob = 0.5 * (1.0 + lax.erf(preact * 0.7071067811865476))
            actives[at, lanes] = (preact * prob).astype(BF16)
            slope = prob + preact * jnp.exp(-0.5 * preact * preact) * 0.3989422804014327
            grad_preact = (grad_hidden * slope).astype(BF16)
            grads[at, lanes] = grad_preact
            grad_normed[at, :] += dot(grad_preact, first[:, units_at], (((1,), (1,)), ((), ())))
            return bias_sum + jnp.sum(grad_preact.astype(F32), axis=0, keepdims=True)

        grad_bias_ref[:, units_at] = lax.fori_loop(
            0, 2, block, jnp.zeros((1, wide), F32), unroll=True
        )

    def sums(start, wide, slot):
        units_at = pl.ds(start, wide)
        lanes = pl.ds(slot * BLOCK, wide)
        sum_second[units_at, :] = dot(actives[:, lanes], cots[...], (((0,), (0,)), ((), ())))
        sum_first[:, units_at] = dot(flipped[...], grads[:, lanes], (((1,), (0,)), ((), ())))

    chunks = [(start, min(BLOCK, hidden - start)) for start in range(0, hidden, BLOCK)]
    for i, (start, wide) in enumerate(chunks):
        chunk(start, wide, i % 2)
        if i:
            sums(*chunks[i - 1], (i - 1) % 2)
    sums(*chunks[-1], (len(chunks) - 1) % 2)

    leaving = []

    def leave(src, dst):
        copy = pltpu.make_async_copy(src, dst, out_sems.at[len(leaving)])
        copy.start()
        leaving.append(copy)

    leave(grad_normed.at[pl.ds(0, half), :], gn_mine_out)

    def narrow(i, _):
        at = pl.ds(aligned(i, tall), tall)
        gn_theirs_ref[at, :] = grad_normed[pl.ds(half + aligned(i, tall), tall), :].astype(BF16)
        return 0

    lax.fori_loop(0, half // tall, narrow, 0)
    leave(gn_theirs_ref, gn_theirs_out)

    def scale_rows(i, total):
        at = pl.ds(aligned(i, tall), tall)
        return total + sum_second[at, :] * second[at, :].astype(F32)

    total = lax.fori_loop(0, hidden // tall, scale_rows, jnp.zeros((tall, channels), F32))
    scale_ref[...] = jnp.sum(total, axis=0, keepdims=True)
    none = jnp.zeros((SUBLANES, LANES), F32)

    def pack_pair(pair, _):
        for e in range(chips):
            tiles = []
            for f in range(2):
                for i in range(PART_TILES):
                    r, c = tile_of(e, i, hidden // LANES)
                    row = pl.multiple_of((2 * pair + f) * own + r * SUBLANES, SUBLANES)
                    tiles.append(
                        sum_first[pl.ds(row, SUBLANES), c * LANES : (c + 1) * LANES]
                        if r * SUBLANES < own
                        else none
                    )
            for i in range(0, len(tiles), 2):
                at = pl.multiple_of(pair * part_rows + i * SUBLANES, tall)
                sums_ref[e, pl.ds(at, tall), :] = jnp.concatenate(tiles[i : i + 2]).astype(BF16)
        return 0

    lax.fori_loop(0, shards // 2, pack_pair, 0)
    for e in range(chips):
        leave(
            sums_ref.at[e, pl.ds(0, first_rows), :], sums_out.at[e, pl.ds(0, first_rows), :]
        )

    def pack_shard(f, _):
        for e in range(chips):
            for i in range(PART_TILES):
                r, c = tile_of(e, i, channels // LANES)
                at = pl.multiple_of(first_rows + f * part_rows + i * tall, tall)
                if r * tall < units:
                    row = pl.multiple_of(f * units + r * tall, tall)
                    value = sum_second[pl.ds(row, tall), c * LANES : (c + 1) * LANES]
                else:
                    value = jnp.zeros((tall, LANES), F32)
                sums_ref[e, pl.ds(at, tall), :] = value.astype(BF16)
        return 0

    lax.fori_loop(0, shards // 2, pack_shard, 0)
    rest = sums_ref.shape[1] - first_rows
    for e in range(chips):
        leave(
            sums_ref.at[e, pl.ds(first_rows, rest), :],
            sums_out.at[e, pl.ds(first_rows, rest), :],
        )
    for copy in leaving:
        copy.wait()


def mlp(core, order, mine, theirs, gb_mine, gb_theirs, bias, second, pieces):
    tokens, channels = mine.shape
    count, hidden = len(pieces), bias.shape[1]
    sums = (second.shape[0], 2 * count * PART_TILES * SUBLANES + second.shape[1], LANES)
    smem = pl.BlockSpec(memory_space=pltpu.SMEM)
    vmem = pl.BlockSpec(memory_space=pltpu.VMEM)
    anywhere = pl.BlockSpec(memory_space=pl.ANY)
    return pl.pallas_call(
        functools.partial(mlp_kernel, count),
        in_specs=[smem, smem] + [anywhere] * 4 + [vmem, vmem] + [anywhere] * count,
        out_specs=[anywhere] * 3 + [vmem] * 2,
        out_shape=[
            jax.ShapeDtypeStruct(sums, BF16),
            jax.ShapeDtypeStruct((tokens, channels), F32),
            jax.ShapeDtypeStruct((tokens, channels), BF16),
            jax.ShapeDtypeStruct((1, hidden), F32),
            jax.ShapeDtypeStruct((1, channels), F32),
        ],
        scratch_shapes=[
            pltpu.VMEM((channels, hidden), BF16),
            pltpu.VMEM((hidden, channels), BF16),
            pltpu.VMEM((channels, hidden), F32),
            pltpu.VMEM((hidden, channels), F32),
            pltpu.VMEM((2 * tokens, channels), BF16),
            pltpu.VMEM((2 * tokens, channels), BF16),
            pltpu.VMEM((channels, 2 * tokens), BF16),
            pltpu.VMEM((2 * tokens, channels), F32),
            pltpu.VMEM((2 * tokens, 2 * BLOCK), BF16),
            pltpu.VMEM((2 * tokens, 2 * BLOCK), BF16),
            pltpu.VMEM(sums, BF16),
            pltpu.VMEM((tokens, channels), BF16),
            pltpu.SemaphoreType.DMA((count,)),
            pltpu.SemaphoreType.DMA((4,)),
            pltpu.SemaphoreType.DMA((2 + 2 * sums[0],)),
        ],
        compiler_params=pltpu.CompilerParams(vmem_limit_bytes=VMEM_LIMIT),
        cost_estimate=pl.CostEstimate(
            flops=20 * tokens * channels * hidden,
            bytes_accessed=12 * hidden * channels,
            transcendentals=4 * tokens * hidden,
        ),
        name="mlp",
    )(core, order, mine, theirs, gb_mine, gb_theirs, bias, second, *pieces)


def unnorm_kernel(gn_ref, gn_other_ref, std_ref, inv_ref, gain_ref, grad_conv_ref, channel_ref):
    step = pl.program_id(0)
    channels = gn_ref.shape[1]
    parts = [slice(c, c + LANES) for c in range(0, channels, LANES)]
    gain = [gain_ref[:, c] for c in parts]
    tall = 32

    @pl.when(step == 0)
    def _():
        channel_ref[...] = jnp.zeros_like(channel_ref)

    def one(i, sums):
        at = pl.ds(pl.multiple_of(i * tall, tall), tall)
        inv = inv_ref[at, :]
        scaled, new = [], []
        for c, lanes in enumerate(parts):
            gn = gn_ref[at, lanes] + gn_other_ref[at, lanes].astype(F32)
            std = std_ref[at, lanes]
            product = gn * std
            gain_sum, shift_sum = sums[2 * c], sums[2 * c + 1]
            for r in range(0, tall, SUBLANES):
                gain_sum = gain_sum + product[r : r + SUBLANES]
                shift_sum = shift_sum + gn[r : r + SUBLANES]
            new += [gain_sum, shift_sum]
            scaled.append((gn * gain[c], product * gain[c], std))
        mean = sum(jnp.sum(v[0], axis=1, keepdims=True) for v in scaled) / channels
        mean_std = sum(jnp.sum(v[1], axis=1, keepdims=True) for v in scaled) / channels
        for c, (v, _, std) in enumerate(scaled):
            grad_conv_ref[at, parts[c]] = inv * (v - mean - std * mean_std)
        return tuple(new)

    zero = jnp.zeros((SUBLANES, LANES), F32)
    sums = lax.fori_loop(0, NORM_BLOCK // tall, one, (zero,) * (2 * len(parts)))
    for c, lanes in enumerate(parts):
        channel_ref[0:1, lanes] += jnp.sum(sums[2 * c], axis=0, keepdims=True)
        channel_ref[1:2, lanes] += jnp.sum(sums[2 * c + 1], axis=0, keepdims=True)


def unnorm(gn, gn_other, std, inv, gain):
    tokens, channels = gn.shape
    block = pl.BlockSpec((NORM_BLOCK, channels), lambda j: (j, 0))
    return pl.pallas_call(
        unnorm_kernel,
        grid=(tokens // NORM_BLOCK,),
        in_specs=[
            block, block, block,
            pl.BlockSpec((NORM_BLOCK, 1), lambda j: (j, 0)),
            whole((1, channels)),
        ],
        out_specs=[block, whole((2, channels))],
        out_shape=[
            jax.ShapeDtypeStruct((tokens, channels), F32),
            jax.ShapeDtypeStruct((2, channels), F32),
        ],
        compiler_params=pltpu.CompilerParams(vmem_limit_bytes=SMALL_VMEM),
        cost_estimate=pl.CostEstimate(
            flops=20 * tokens * channels, bytes_accessed=14 * tokens * channels, transcendentals=0
        ),
        name="unnorm",
    )(gn, gn_other, std, inv, gain)


def load_grads(grad_ref, rows, grad_minor, groups, tokens):
    rows[:tokens, :] = grad_ref[...]
    if rows.shape[0] > tokens:
        rows[tokens:, :] = jnp.zeros((rows.shape[0] - tokens, LANES), F32)
    to_patch_minor(rows, grad_minor, groups)


def taps_kernel(
    slots, x_ref, grad_ref, _after, _buffer, grad_taps_ref, rows, minor, grad_minor, tap_sums
):
    groups = rows.shape[0] // (SUBLANES * SPOTS)
    load_grads(grad_ref, rows, grad_minor, groups, slots * SPOTS)

    def load(slot, _):
        rows[pl.ds(pl.multiple_of(slot * SPOTS, SPOTS), SPOTS), :] = (
            x_ref[slot].astype(F32).reshape(SPOTS, LANES)
        )
        return 0

    lax.fori_loop(0, slots, load, 0)
    to_patch_minor(rows, minor, groups)

    def taps(group, _):
        for a in range(TAPS):
            sums = [jnp.where(group == 0, 0.0, tap_sums[a * TAPS + b]) for b in range(TAPS)]
            for p in range(SIDE):
                row = p + a - REACH
                if not 0 <= row < SIDE:
                    continue
                values = [minor[group * SPOTS + row * SIDE + q] for q in range(SIDE)]
                grads = [grad_minor[group * SPOTS + p * SIDE + q] for q in range(SIDE)]
                for b in range(TAPS):
                    for q in range(SIDE):
                        col = q + b - REACH
                        if 0 <= col < SIDE:
                            sums[b] = sums[b] + grads[q] * values[col]
            for b in range(TAPS):
                tap_sums[a * TAPS + b] = sums[b]
        return 0

    lax.fori_loop(0, groups, taps, 0)
    for tap in range(TAPS * TAPS):
        grad_taps_ref[tap : tap + 1, :] = jnp.sum(tap_sums[tap], axis=0, keepdims=True)


def taps_part(part, x, grad_conv, after, buffer):
    slots, channels, tokens, groups, padded = shapes_of(x)
    base = part * GROUP_STEPS
    anywhere = pl.BlockSpec(memory_space=pl.ANY)
    if buffer is None:
        buffer, aliases = after, {}
    else:
        aliases = {3: 0}
    return pl.pallas_call(
        functools.partial(taps_kernel, slots),
        grid=(GROUP_STEPS,),
        in_specs=[
            pl.BlockSpec((slots, SIDE, SIDE, LANES), lambda j: (0, 0, 0, j + base)),
            pl.BlockSpec((tokens, LANES), lambda j: (0, j + base)),
            anywhere,
            anywhere,
        ],
        out_specs=pl.BlockSpec((TAPS * TAPS, LANES), lambda j: (0, j + base)),
        out_shape=jax.ShapeDtypeStruct((TAPS * TAPS, channels), F32),
        input_output_aliases=aliases,
        scratch_shapes=[
            pltpu.VMEM((padded, LANES), F32),
            pltpu.VMEM((groups * SPOTS, SUBLANES, LANES), F32),
            pltpu.VMEM((groups * SPOTS, SUBLANES, LANES), F32),
            pltpu.VMEM((TAPS * TAPS, SUBLANES, LANES), F32),
        ],
        compiler_params=pltpu.CompilerParams(vmem_limit_bytes=SMALL_VMEM),
        cost_estimate=pl.CostEstimate(
            flops=2 * 49 * tokens * LANES * GROUP_STEPS,
            bytes_accessed=6 * tokens * LANES * GROUP_STEPS,
            transcendentals=0,
        ),
        name="taps",
    )(x, grad_conv, after, buffer)


def back_kernel(
    slots, g_ref, grad_ref, count_ref, taps_ref, _after, _buffer, in_grad_ref,
    rows, grad_minor, spread, result,
):
    groups = rows.shape[0] // (SUBLANES * SPOTS)
    spread_taps(taps_ref, spread)
    load_grads(grad_ref, rows, grad_minor, groups, slots * SPOTS)

    def convolve(group, _):
        def emit(spot, value):
            result[pl.ds(group * SUBLANES * SPOTS + spot, SUBLANES, stride=SPOTS), :] = value

        conv_rows(grad_minor, spread, group, True, emit)
        return 0

    lax.fori_loop(0, groups, convolve, 0)
    count = count_ref[0, 0]

    def finish(slot, _):
        live = jnp.where(slot < count, 1.0, 0.0)
        g = g_ref[slot].astype(F32) * live
        at = pl.ds(pl.multiple_of(slot * SPOTS, SPOTS), SPOTS)
        in_grad_ref[slot] = g + result[at, :].reshape(SIDE, SIDE, LANES)
        return 0

    lax.fori_loop(0, slots, finish, 0)


def back_part(part, g, grad_conv, count, taps, after, buffer):
    slots, channels, tokens, groups, padded = shapes_of(g)
    base = part * GROUP_STEPS
    anywhere = pl.BlockSpec(memory_space=pl.ANY)
    if buffer is None:
        buffer, aliases = after, {}
    else:
        aliases = {5: 0}
    return pl.pallas_call(
        functools.partial(back_kernel, slots),
        grid=(GROUP_STEPS,),
        in_specs=[
            pl.BlockSpec((slots, SIDE, SIDE, LANES), lambda j: (0, 0, 0, j + base)),
            pl.BlockSpec((tokens, LANES), lambda j: (0, j + base)),
            pl.BlockSpec(memory_space=pltpu.SMEM),
            pl.BlockSpec((TAPS * TAPS, LANES), lambda j: (0, j + base)),
            anywhere,
            anywhere,
        ],
        out_specs=pl.BlockSpec((slots, SIDE, SIDE, LANES), lambda j: (0, 0, 0, j + base)),
        out_shape=jax.ShapeDtypeStruct((slots, SIDE, SIDE, channels), F32),
        input_output_aliases=aliases,
        scratch_shapes=[
            pltpu.VMEM((padded, LANES), F32),
            pltpu.VMEM((groups * SPOTS, SUBLANES, LANES), F32),
            pltpu.VMEM((TAPS * TAPS, SUBLANES, LANES), F32),
            pltpu.VMEM((padded, LANES), F32),
        ],
        compiler_params=pltpu.CompilerParams(vmem_limit_bytes=SMALL_VMEM),
        cost_estimate=pl.CostEstimate(
            flops=2 * 49 * tokens * LANES * GROUP_STEPS,
            bytes_accessed=10 * tokens * LANES * GROUP_STEPS,
            transcendentals=0,
        ),
        name="back",
    )(g, grad_conv, count, taps, after, buffer)


def device_index(x, y, z, core):
    high, low = divmod(y % Y, 2)
    return ((x % X) * 4 + high * 2 + core) * (2 * Z) + (z % Z) * 2 + low


def move(value, dy=0, dz=0, flip=0):
    pairs = [
        (device_index(x, y, z, core), device_index(x, y + dy, z + dz, core ^ flip))
        for x in range(X)
        for y in range(Y)
        for z in range(Z)
        for core in range(2)
    ]
    return lax.ppermute(value, AXES, pairs)


def gather_pieces(piece, z, low, between):
    other = lax.ppermute(piece, "fsdp", [(i, i ^ 1) for i in range(2 * Z)])
    pair = jnp.concatenate([piece, other])
    right, left = move(pair, dz=1), move(pair, dz=-1)
    right, left, made = between(right, left)
    pieces, away = [pair, right, left], [0, Z - 1, 1]
    for step in range(2, Z // 2 + 1):
        right = move(right, dz=1)
        pieces.append(right)
        away.append(Z - step)
        if step < Z // 2:
            left = move(left, dz=-1)
            pieces.append(left)
            away.append(step)
    order = [(z + s) % Z * 2 + (low ^ parity) for s in away for parity in range(2)]
    return jnp.stack(order).astype(jnp.int32), pieces, made


def copies_kernel(kept_ref, swapped_ref, _right, _left, out_ref, _right_out, _left_out):
    def shard(f, _):
        both = [kept_ref[f].astype(F32), swapped_ref[f].astype(F32)]
        both = jnp.concatenate(both).astype(BF16)
        rows = both.shape[0]
        for e in range(out_ref.shape[0]):
            out_ref[e, pl.ds(pl.multiple_of(f * rows, rows), rows), :] = both
        return 0

    lax.fori_loop(0, kept_ref.shape[0], shard, 0)


def copies(chips, kept, swapped, right, left):
    shards, rows, lanes = kept.shape
    vmem = pl.BlockSpec(memory_space=pltpu.VMEM)
    anywhere = pl.BlockSpec(memory_space=pl.ANY)
    return pl.pallas_call(
        copies_kernel,
        in_specs=[vmem, vmem, anywhere, anywhere],
        out_specs=[vmem, anywhere, anywhere],
        out_shape=[
            jax.ShapeDtypeStruct((chips, shards * 2 * rows, lanes), BF16),
            jax.ShapeDtypeStruct(right.shape, BF16),
            jax.ShapeDtypeStruct(left.shape, BF16),
        ],
        input_output_aliases={2: 1, 3: 2},
        compiler_params=pltpu.CompilerParams(vmem_limit_bytes=SMALL_VMEM),
        name="copies",
    )(kept, swapped, right, left)


def add_up_kernel(terms_ref, _after, out_ref):
    tall = 8 * SUBLANES

    def rows(i, _):
        at = pl.ds(pl.multiple_of(i * tall, tall), tall)
        total = terms_ref[0, at, :].astype(F32)
        for e in range(1, terms_ref.shape[0]):
            total = total + terms_ref[e, at, :].astype(F32)
        out_ref[at, :] = total.astype(BF16)
        return 0

    lax.fori_loop(0, terms_ref.shape[1] // tall, rows, 0, unroll=2)


def add_up(terms, after):
    return pl.pallas_call(
        add_up_kernel,
        in_specs=[
            pl.BlockSpec(memory_space=pltpu.VMEM),
            pl.BlockSpec(memory_space=pl.ANY),
        ],
        out_shape=jax.ShapeDtypeStruct(terms.shape[1:], BF16),
        compiler_params=pltpu.CompilerParams(vmem_limit_bytes=SMALL_VMEM),
        name="add_up",
    )(terms, after)


def finish_kernel(
    factor, place_ref, mine_ref, theirs_ref, first_ref, second_ref, small_ref
):
    core, side = place_ref[0], place_ref[1]
    small_rows = PART_TILES * 2 * SUBLANES
    half = small_rows // 2
    wide = first_ref.shape[1] // 2 // LANES
    small = None
    for e in range(mine_ref.shape[0]):
        mine, theirs = mine_ref[e].astype(F32), theirs_ref[e].astype(F32)
        for k in range(2):
            part = jnp.where(core == k, mine[:half], theirs[:half]) * factor
            for i in range(PART_TILES):
                r, c = tile_of(e, i, wide)
                if r * SUBLANES < first_ref.shape[0]:
                    lane = (k * wide + c) * LANES
                    first_ref[r * SUBLANES : (r + 1) * SUBLANES, lane : lane + LANES] = part[
                        i * SUBLANES : (i + 1) * SUBLANES
                    ]
        more = mine[small_rows:] + theirs[small_rows:]
        small = more if small is None else small + more
        mine, theirs = mine[half:small_rows], theirs[half:small_rows]
        part = jnp.concatenate(
            [jnp.where(core == side, mine, theirs), jnp.where(core == side, theirs, mine)]
        )
        part = part * factor
        for i in range(PART_TILES):
            r, c = tile_of(e, i, second_ref.shape[1] // LANES)
            if r * 2 * SUBLANES < second_ref.shape[0]:
                second_ref[r * 2 * SUBLANES : (r + 1) * 2 * SUBLANES, c * LANES : (c + 1) * LANES] = (
                    part[i * 2 * SUBLANES : (i + 1) * 2 * SUBLANES]
                )
    small_ref[...] = small * factor


def finish(place, mine, theirs, first_shape, second_shape, factor):
    small = (mine.shape[1] - PART_TILES * 2 * SUBLANES, LANES)
    vmem = pl.BlockSpec(memory_space=pltpu.VMEM)
    return pl.pallas_call(
        functools.partial(finish_kernel, factor),
        in_specs=[pl.BlockSpec(memory_space=pltpu.SMEM), vmem, vmem],
        out_shape=[
            jax.ShapeDtypeStruct(first_shape, F32),
            jax.ShapeDtypeStruct(second_shape, F32),
            jax.ShapeDtypeStruct(small, F32),
        ],
        compiler_params=pltpu.CompilerParams(vmem_limit_bytes=SMALL_VMEM),
        name="finish",
    )(place, mine, theirs)


def pack(rows):
    count, width = rows.shape[-2:]
    half = -(-count // 2)
    lead = [(0, 0)] * (rows.ndim - 2)
    rows = jnp.pad(rows, lead + [(0, 2 * half - count), (0, 0)])
    rows = jnp.concatenate([rows[..., :half, :], rows[..., half:, :]], axis=-1)
    return jnp.pad(rows, lead + [(0, -half % (2 * SUBLANES)), (0, LANES - 2 * width)])


def unpack(packed, count, width):
    half = -(-count // 2)
    rows = [packed[..., :half, :width], packed[..., :half, width : 2 * width]]
    return jnp.concatenate(rows, axis=-2)[..., :count, :]


def local(
    patches,
    out_grad,
    row_counts,
    dw_kernel,
    ln_gain,
    ln_bias,
    w_first,
    first_bias,
    w_second,
    layer_scale,
):
    fsdp, dp = lax.axis_size("fsdp"), lax.axis_size("dp")
    own = ln_gain.shape[0]
    units = first_bias.shape[0]
    channels, hidden = own * fsdp, units * fsdp
    mine = hidden // 2
    tap_count = dw_kernel.shape[0]
    dp_index, fsdp_index = lax.axis_index("dp"), lax.axis_index("fsdp")
    core = dp_index % 2
    z, low = fsdp_index // 2, fsdp_index % 2

    chip, chips = dp_index // 2, dp // 2
    side = fsdp_index // (fsdp // 2)
    same_core = [[2 * i + c for i in range(chips)] for c in range(2)]
    flat = (PART_TILES * SUBLANES, LANES)

    tall, across = units // (2 * SUBLANES), channels // LANES
    tiles = w_second.reshape(tall, 2 * SUBLANES, across, LANES).transpose(0, 2, 1, 3)
    tiles = tiles.reshape(tall * across, 2 * SUBLANES, LANES)
    tiles = jnp.pad(tiles, ((0, chips * PART_TILES - tall * across), (0, 0), (0, 0)))
    tiles = tiles.reshape(chips * 2, *flat)
    tiles = lax.dynamic_index_in_dim(tiles, 2 * chip + (core ^ side), 0, keepdims=False)
    vectors = [ln_gain[None], ln_bias[None], layer_scale[None], first_bias.reshape(-1, own)]
    small = jnp.concatenate([dw_kernel] + vectors)
    lines = small.shape[0]
    small = jnp.concatenate([tiles, pack(small)])
    small = lax.all_to_all(
        jnp.broadcast_to(small, (fsdp,) + small.shape), "fsdp", 0, 0, tiled=True
    )
    tiles, small = small[:, : flat[0]], unpack(small[:, flat[0] :], lines, own)
    kept = lax.dynamic_slice_in_dim(tiles, core * (fsdp // 2), fsdp // 2)
    swapped = move(lax.dynamic_slice_in_dim(tiles, (1 - core) * (fsdp // 2), fsdp // 2), flip=1)

    def between(right, left):
        made, right, left = copies(chips, kept, swapped, right, left)
        made = lax.all_to_all(made, "dp", 0, 0, tiled=True, axis_index_groups=same_core)
        return right, left, made

    part = lax.dynamic_slice_in_dim(w_first, core * mine, mine, 1)
    part = [part[:, k * CUT : (k + 1) * CUT] for k in range(mine // CUT)]
    order, pieces, second = gather_pieces(jnp.concatenate(part), z, low, between)

    taps = small[:, :tap_count].transpose(1, 0, 2).reshape(tap_count, channels).astype(F32)
    gain, shift, scale = (
        small[:, tap_count + i].reshape(1, channels).astype(F32) for i in range(3)
    )
    bias = small[:, tap_count + 3 :].reshape(1, hidden).astype(F32)
    bias = lax.dynamic_slice_in_dim(bias, core * mine, mine, 1)

    x, g = patches[0], out_grad[0]
    conv = conv_part(0, x, taps, pieces[1], None)
    conv = conv_part(1, x, taps, pieces[4], conv)
    conv = conv_part(2, x, taps, pieces[6], conv)
    normed, std, inv, gb = norm(conv, g, row_counts, gain, shift, scale, pieces[7])
    normed_other, gb_other = move(normed, flip=1), move(gb, flip=1)
    terms, gn_mine, gn_theirs, grad_bias, scale_sum = mlp(
        core.reshape(1), order, normed, normed_other, gb, gb_other, bias, second, pieces
    )
    gn_other = move(gn_theirs, flip=1)
    scale_sum = scale_sum / scale
    grad_conv, channel_sums = unnorm(gn_mine, gn_other, std, inv, gain)
    grad_taps = taps_part(0, x, grad_conv, terms, None)
    grad_taps = taps_part(1, x, grad_conv, terms, grad_taps)
    grad_taps = taps_part(2, x, grad_conv, terms, grad_taps)
    in_grad = back_part(0, g, grad_conv, row_counts, taps, terms, None)
    in_grad = back_part(1, g, grad_conv, row_counts, taps, terms, in_grad)
    in_grad = back_part(2, g, grad_conv, row_counts, taps, terms, in_grad)

    terms = lax.all_to_all(terms, "dp", 0, 0, tiled=True, axis_index_groups=same_core)
    terms = add_up(terms, in_grad)
    first = terms[: fsdp * flat[0]].reshape((fsdp,) + flat)
    second = terms[fsdp * flat[0] :].reshape((fsdp // 2, 2) + flat)
    swapped = move(second[:, 1], flip=1)
    second = jnp.where(
        core == 0,
        jnp.concatenate([second[:, 0], swapped]),
        jnp.concatenate([swapped, second[:, 0]]),
    )
    sums = jnp.concatenate([grad_taps, channel_sums, scale_sum], axis=0)
    sums = sums.reshape(sums.shape[0], fsdp, own).transpose(1, 0, 2)
    grad_bias = jnp.concatenate([grad_bias, grad_bias], axis=1).reshape(fsdp, -1, own)
    computed = (jnp.arange(fsdp, dtype=jnp.int32) // (fsdp // 2) == core)[:, None, None]
    sums = jnp.concatenate([sums, jnp.where(computed, grad_bias, 0.0)], axis=1)
    terms = jnp.concatenate([first, second, pack(sums.astype(BF16))], axis=1)
    terms = lax.all_to_all(terms, "fsdp", 0, 0, tiled=True)
    terms = jnp.sum(terms.astype(F32), axis=0).astype(BF16)
    terms = lax.all_to_all(
        jnp.broadcast_to(terms[None], (chips,) + terms.shape),
        "dp", 0, 0, tiled=True, axis_index_groups=same_core,
    )
    factor = 1.0 / math.sqrt(fsdp * dp * ROWS * SPOTS)
    first, second, sums = finish(
        jnp.stack([core, side]).astype(jnp.int32),
        terms,
        move(terms, flip=1),
        (own, hidden),
        (units, channels),
        factor,
    )
    sums = unpack(sums, lines, own)
    return (
        in_grad[None],
        first,
        second,
        sums[:tap_count],
        sums[tap_count + 3 :].reshape(units),
        sums[tap_count : tap_count + 3],
    )


def solution(mesh):
    placed = (
        P("fsdp", "dp", None, None, None),
        P("fsdp", "dp", None, None, None),
        P("fsdp", "dp"),
        P(None, "fsdp"),
        P("fsdp"),
        P("fsdp"),
        P("fsdp", None),
        P("fsdp"),
        P("fsdp", None),
        P("fsdp"),
    )
    return jax.shard_map(
        local,
        mesh=mesh,
        in_specs=placed,
        out_specs=(
            P("fsdp", "dp", None, None, None),
            P("fsdp", None),
            P("fsdp", None),
            P(None, "fsdp"),
            P("fsdp"),
            P(None, "fsdp"),
        ),
        check_vma=False,
    )
```

```python
import functools
import math

import jax
import jax.numpy as jnp
from jax import lax
from jax.experimental import pallas as pl
from jax.experimental.pallas import tpu as pltpu
from jax.sharding import PartitionSpec as P

ROWS = 8
LANES = 128
SUBLANES = 8
SIDE = 8
SPOTS = SIDE * SIDE
REACH = 3
TAPS = 7
BLOCK = 256
NORM_BLOCK = 128
PART_TILES = 7
GROUP_STEPS = 2
CUT = 384
AXES = ("dp", "fsdp")
X, Y, Z = 4, 4, 8
BF16, F32 = jnp.bfloat16, jnp.float32
VMEM_LIMIT = 56 * 1024 * 1024
SMALL_VMEM = 24 * 1024 * 1024


def whole(shape):
    return pl.BlockSpec(shape, lambda *_: (0,) * len(shape))


def spread_taps(taps_ref, spread):
    for tap in range(TAPS * TAPS):
        spread[tap] = jnp.broadcast_to(taps_ref[tap : tap + 1, :], (SUBLANES, LANES))


def to_patch_minor(rows, out, groups):
    def one(spot, _):
        for group in range(groups):
            out[group * SPOTS + spot] = rows[
                pl.ds(group * SUBLANES * SPOTS + spot, SUBLANES, stride=SPOTS), :
            ]
        return 0

    lax.fori_loop(0, SPOTS, one, 0, unroll=8)


def conv_rows(src, spread, group, flip, emit):
    for p in range(SIDE):
        sums = [None] * SIDE
        for a in range(TAPS):
            row = p + a - REACH
            if not 0 <= row < SIDE:
                continue
            values = [src[group * SPOTS + row * SIDE + q] for q in range(SIDE)]
            for b in range(TAPS):
                tap = a * TAPS + b
                weight = spread[TAPS * TAPS - 1 - tap if flip else tap]
                for q in range(SIDE):
                    col = q + b - REACH
                    if 0 <= col < SIDE:
                        term = values[col] * weight
                        sums[q] = term if sums[q] is None else sums[q] + term
        for q in range(SIDE):
            emit(p * SIDE + q, sums[q])


def conv_kernel(
    slots, x_ref, taps_ref, _after, _buffer, out_ref, rows, minor, spread, conv
):
    groups = rows.shape[0] // (SUBLANES * SPOTS)
    spread_taps(taps_ref, spread)

    def load(slot, _):
        rows[pl.ds(pl.multiple_of(slot * SPOTS, SPOTS), SPOTS), :] = (
            x_ref[slot].astype(F32).reshape(SPOTS, LANES)
        )
        return 0

    lax.fori_loop(0, slots, load, 0)
    to_patch_minor(rows, minor, groups)

    def convolve(group, _):
        def emit(spot, value):
            conv[pl.ds(group * SUBLANES * SPOTS + spot, SUBLANES, stride=SPOTS), :] = value

        conv_rows(minor, spread, group, False, emit)
        return 0

    lax.fori_loop(0, groups, convolve, 0)
    out_ref[...] = conv[: slots * SPOTS, :]


def shapes_of(x):
    slots, channels = x.shape[0], x.shape[3]
    groups = -(-slots // SUBLANES)
    return slots, channels, slots * SPOTS, groups, groups * SUBLANES * SPOTS


def conv_part(part, x, taps, after, buffer):
    slots, channels, tokens, groups, padded = shapes_of(x)
    base = part * GROUP_STEPS
    anywhere = pl.BlockSpec(memory_space=pl.ANY)
    if buffer is None:
        buffer, aliases = after, {}
    else:
        aliases = {3: 0}
    return pl.pallas_call(
        functools.partial(conv_kernel, slots),
        grid=(GROUP_STEPS,),
        in_specs=[
            pl.BlockSpec((slots, SIDE, SIDE, LANES), lambda j: (0, 0, 0, j + base)),
            pl.BlockSpec((TAPS * TAPS, LANES), lambda j: (0, j + base)),
            anywhere,
            anywhere,
        ],
        out_specs=pl.BlockSpec((tokens, LANES), lambda j: (0, j + base)),
        out_shape=jax.ShapeDtypeStruct((tokens, channels), F32),
        input_output_aliases=aliases,
        scratch_shapes=[
            pltpu.VMEM((padded, LANES), F32),
            pltpu.VMEM((groups * SPOTS, SUBLANES, LANES), F32),
            pltpu.VMEM((TAPS * TAPS, SUBLANES, LANES), F32),
            pltpu.VMEM((padded, LANES), F32),
        ],
        compiler_params=pltpu.CompilerParams(vmem_limit_bytes=SMALL_VMEM),
        cost_estimate=pl.CostEstimate(
            flops=2 * 49 * tokens * LANES * GROUP_STEPS,
            bytes_accessed=6 * tokens * LANES * GROUP_STEPS,
            transcendentals=0,
        ),
        name="conv",
    )(x, taps, after, buffer)


def norm_kernel(
    conv_ref, g_ref, count_ref, gain_ref, shift_ref, scale_ref, _after,
    normed_ref, std_ref, inv_ref, gb_ref,
):
    step = pl.program_id(0)
    count = count_ref[0, 0]
    channels = conv_ref.shape[1]
    parts = [slice(c, c + LANES) for c in range(0, channels, LANES)]
    gain, shift, scale = ([ref[:, c] for c in parts] for ref in (gain_ref, shift_ref, scale_ref))
    tall = 32

    def norm(i, _):
        at = pl.ds(pl.multiple_of(i * tall, tall), tall)
        values = [conv_ref[at, c] for c in parts]
        mean = sum(jnp.sum(v, axis=1, keepdims=True) for v in values) / channels
        values = [v - mean for v in values]
        var = sum(jnp.sum(v * v, axis=1, keepdims=True) for v in values) / channels
        inv = lax.rsqrt(var + 1e-06)
        inv_ref[at, :] = inv
        for c, v in enumerate(values):
            std = v * inv
            std_ref[at, parts[c]] = std
            normed_ref[at, parts[c]] = (std * gain[c] + shift[c]).astype(BF16)
        return 0

    lax.fori_loop(0, NORM_BLOCK // tall, norm, 0, unroll=2)
    for slot in range(NORM_BLOCK // SPOTS):
        live = jnp.where(step * (NORM_BLOCK // SPOTS) + slot < count, 1.0, 0.0)
        for c, lanes in enumerate(parts):
            g = g_ref[slot, :, :, lanes].astype(F32).reshape(SPOTS, LANES)
            gb_ref[slot * SPOTS : (slot + 1) * SPOTS, lanes] = (g * (scale[c] * live)).astype(BF16)


def norm(conv, g, count, gain, shift, scale, after):
    tokens, channels = conv.shape
    block = pl.BlockSpec((NORM_BLOCK, channels), lambda j: (j, 0))
    vector = whole((1, channels))
    return pl.pallas_call(
        norm_kernel,
        grid=(tokens // NORM_BLOCK,),
        in_specs=[
            block,
            pl.BlockSpec((NORM_BLOCK // SPOTS, SIDE, SIDE, channels), lambda j: (j, 0, 0, 0)),
            pl.BlockSpec(memory_space=pltpu.SMEM),
            vector, vector, vector,
            pl.BlockSpec(memory_space=pl.ANY),
        ],
        out_specs=[block, block, pl.BlockSpec((NORM_BLOCK, 1), lambda j: (j, 0)), block],
        out_shape=[
            jax.ShapeDtypeStruct((tokens, channels), BF16),
            jax.ShapeDtypeStruct((tokens, channels), F32),
            jax.ShapeDtypeStruct((tokens, 1), F32),
            jax.ShapeDtypeStruct((tokens, channels), BF16),
        ],
        compiler_params=pltpu.CompilerParams(vmem_limit_bytes=SMALL_VMEM),
        cost_estimate=pl.CostEstimate(
            flops=20 * tokens * channels, bytes_accessed=14 * tokens * channels, transcendentals=0
        ),
        name="norm",
    )(conv, g, count, gain, shift, scale, after)


def tile_of(part, i, across):
    return divmod(part * PART_TILES + i, across)


def aligned(value, to):
    return pl.multiple_of(value * to, to)


def clear(ref):
    tall = 2 * SUBLANES

    def rows(i, _):
        ref[pl.ds(aligned(i, tall), tall), :] = jnp.zeros((tall, ref.shape[1]), F32)
        return 0

    lax.fori_loop(0, ref.shape[0] // tall, rows, 0)


def mlp_kernel(
    count, core_ref, order_ref, mine_ref, theirs_ref, gb_mine_ref, gb_theirs_ref, bias_ref,
    second_ref, *refs,
):
    pieces = refs[:count]
    (
        sums_out, gn_mine_out, gn_theirs_out, grad_bias_ref, scale_ref,
        first, second, sum_first, sum_second, tokens, cots, flipped, grad_normed,
        actives, grads, sums_ref, gn_theirs_ref, sems, more_sems, out_sems,
    ) = refs[count:]
    channels, hidden = first.shape
    half = mine_ref.shape[0]
    chips = second_ref.shape[0]
    cuts = hidden // CUT
    own = pieces[0].shape[0] // (2 * cuts)
    shards = channels // own
    units = hidden // (shards // 2)
    first_rows = shards * PART_TILES * SUBLANES
    part_rows = PART_TILES * 2 * SUBLANES
    tall = 2 * SUBLANES
    dot = functools.partial(lax.dot_general, preferred_element_type=F32)

    loads = [
        pltpu.make_async_copy(src, dst.at[pl.ds(row, half), :], more_sems.at[i])
        for i, (src, dst, row) in enumerate(
            (
                (mine_ref, tokens, 0),
                (theirs_ref, tokens, half),
                (gb_mine_ref, cots, 0),
                (gb_theirs_ref, cots, half),
            )
        )
    ]
    for i, piece in enumerate(pieces):
        for parity in range(2):
            f = order_ref[2 * i + parity]
            for k in range(cuts):
                loads.append(
                    pltpu.make_async_copy(
                        piece.at[pl.ds((parity * cuts + k) * own, own), :],
                        first.at[pl.ds(aligned(f, own), own), pl.ds(k * CUT, CUT)],
                        sems.at[i],
                    )
                )
    for load in loads:
        load.start()

    def unpack_shard(f, _):
        for e in range(chips):
            for i in range(PART_TILES):
                r, c = tile_of(e, i, channels // LANES)
                if r * tall < units:
                    second[
                        pl.ds(pl.multiple_of(f * units + r * tall, tall), tall),
                        c * LANES : (c + 1) * LANES,
                    ] = second_ref[
                        e, pl.ds(pl.multiple_of(f * part_rows + i * tall, tall), tall), :
                    ]
        return 0

    lax.fori_loop(0, shards // 2, unpack_shard, 0)
    clear(grad_normed)
    for load in loads:
        load.wait()

    def flip(j, _):
        at = pl.ds(aligned(j, BLOCK), BLOCK)
        flipped[:, at] = tokens[at, :].T
        return 0

    lax.fori_loop(0, 2 * half // BLOCK, flip, 0)

    def chunk(start, wide, slot):
        units_at = pl.ds(start, wide)
        lanes = pl.ds(slot * BLOCK, wide)

        def block(j, bias_sum):
            at = pl.ds(aligned(j, half), half)
            preact = dot(tokens[at, :], first[:, units_at], (((1,), (0,)), ((), ())))
            preact = preact + bias_ref[:, units_at]
            grad_hidden = dot(cots[at, :], second[units_at, :], (((1,), (1,)), ((), ())))
            prob = 0.5 * (1.0 + lax.erf(preact * 0.7071067811865476))
            actives[at, lanes] = (preact * prob).astype(BF16)
            slope = prob + preact * jnp.exp(-0.5 * preact * preact) * 0.3989422804014327
            grad_preact = (grad_hidden * slope).astype(BF16)
            grads[at, lanes] = grad_preact
            grad_normed[at, :] += dot(grad_preact, first[:, units_at], (((1,), (1,)), ((), ())))
            return bias_sum + jnp.sum(grad_preact.astype(F32), axis=0, keepdims=True)

        grad_bias_ref[:, units_at] = lax.fori_loop(
            0, 2, block, jnp.zeros((1, wide), F32)
        )

    def sums(start, wide, slot):
        units_at = pl.ds(start, wide)
        lanes = pl.ds(slot * BLOCK, wide)
        sum_second[units_at, :] = dot(actives[:, lanes], cots[...], (((0,), (0,)), ((), ())))
        sum_first[:, units_at] = dot(flipped[...], grads[:, lanes], (((1,), (0,)), ((), ())))

    def whole_chunk(h, _):
        chunk(aligned(h, BLOCK), BLOCK, 0)
        sums(aligned(h, BLOCK), BLOCK, 0)
        return 0

    lax.fori_loop(0, hidden // BLOCK, whole_chunk, 0)
    if hidden % BLOCK:
        chunk(hidden // BLOCK * BLOCK, hidden % BLOCK, 0)
        sums(hidden // BLOCK * BLOCK, hidden % BLOCK, 0)

    leaving = []

    def leave(src, dst):
        copy = pltpu.make_async_copy(src, dst, out_sems.at[len(leaving)])
        copy.start()
        leaving.append(copy)

    leave(grad_normed.at[pl.ds(0, half), :], gn_mine_out)

    def narrow(i, _):
        at = pl.ds(aligned(i, tall), tall)
        gn_theirs_ref[at, :] = grad_normed[pl.ds(half + aligned(i, tall), tall), :].astype(BF16)
        return 0

    lax.fori_loop(0, half // tall, narrow, 0)
    leave(gn_theirs_ref, gn_theirs_out)

    def scale_rows(i, total):
        at = pl.ds(aligned(i, tall), tall)
        return total + sum_second[at, :] * second[at, :].astype(F32)

    total = lax.fori_loop(0, hidden // tall, scale_rows, jnp.zeros((tall, channels), F32))
    scale_ref[...] = jnp.sum(total, axis=0, keepdims=True)
    none = jnp.zeros((SUBLANES, LANES), F32)

    def pack_pair(pair, _):
        for e in range(chips):
            tiles = []
            for f in range(2):
                for i in range(PART_TILES):
                    r, c = tile_of(e, i, hidden // LANES)
                    row = pl.multiple_of((2 * pair + f) * own + r * SUBLANES, SUBLANES)
                    tiles.append(
                        sum_first[pl.ds(row, SUBLANES), c * LANES : (c + 1) * LANES]
                        if r * SUBLANES < own
                        else none
                    )
            for i in range(0, len(tiles), 2):
                at = pl.multiple_of(pair * part_rows + i * SUBLANES, tall)
                sums_ref[e, pl.ds(at, tall), :] = jnp.concatenate(tiles[i : i + 2]).astype(BF16)
        return 0

    lax.fori_loop(0, shards // 2, pack_pair, 0)
    for e in range(chips):
        leave(
            sums_ref.at[e, pl.ds(0, first_rows), :], sums_out.at[e, pl.ds(0, first_rows), :]
        )

    def pack_shard(f, _):
        for e in range(chips):
            for i in range(PART_TILES):
                r, c = tile_of(e, i, channels // LANES)
                at = pl.multiple_of(first_rows + f * part_rows + i * tall, tall)
                if r * tall < units:
                    row = pl.multiple_of(f * units + r * tall, tall)
                    value = sum_second[pl.ds(row, tall), c * LANES : (c + 1) * LANES]
                else:
                    value = jnp.zeros((tall, LANES), F32)
                sums_ref[e, pl.ds(at, tall), :] = value.astype(BF16)
        return 0

    lax.fori_loop(0, shards // 2, pack_shard, 0)
    rest = sums_ref.shape[1] - first_rows
    for e in range(chips):
        leave(
            sums_ref.at[e, pl.ds(first_rows, rest), :],
            sums_out.at[e, pl.ds(first_rows, rest), :],
        )
    for copy in leaving:
        copy.wait()


def mlp(core, order, mine, theirs, gb_mine, gb_theirs, bias, second, pieces):
    tokens, channels = mine.shape
    count, hidden = len(pieces), bias.shape[1]
    sums = (second.shape[0], 2 * count * PART_TILES * SUBLANES + second.shape[1], LANES)
    smem = pl.BlockSpec(memory_space=pltpu.SMEM)
    vmem = pl.BlockSpec(memory_space=pltpu.VMEM)
    anywhere = pl.BlockSpec(memory_space=pl.ANY)
    return pl.pallas_call(
        functools.partial(mlp_kernel, count),
        in_specs=[smem, smem] + [anywhere] * 4 + [vmem, vmem] + [anywhere] * count,
        out_specs=[anywhere] * 3 + [vmem] * 2,
        out_shape=[
            jax.ShapeDtypeStruct(sums, BF16),
            jax.ShapeDtypeStruct((tokens, channels), F32),
            jax.ShapeDtypeStruct((tokens, channels), BF16),
            jax.ShapeDtypeStruct((1, hidden), F32),
            jax.ShapeDtypeStruct((1, channels), F32),
        ],
        scratch_shapes=[
            pltpu.VMEM((channels, hidden), BF16),
            pltpu.VMEM((hidden, channels), BF16),
            pltpu.VMEM((channels, hidden), F32),
            pltpu.VMEM((hidden, channels), F32),
            pltpu.VMEM((2 * tokens, channels), BF16),
            pltpu.VMEM((2 * tokens, channels), BF16),
            pltpu.VMEM((channels, 2 * tokens), BF16),
            pltpu.VMEM((2 * tokens, channels), F32),
            pltpu.VMEM((2 * tokens, BLOCK), BF16),
            pltpu.VMEM((2 * tokens, BLOCK), BF16),
            pltpu.VMEM(sums, BF16),
            pltpu.VMEM((tokens, channels), BF16),
            pltpu.SemaphoreType.DMA((count,)),
            pltpu.SemaphoreType.DMA((4,)),
            pltpu.SemaphoreType.DMA((2 + 2 * sums[0],)),
        ],
        compiler_params=pltpu.CompilerParams(vmem_limit_bytes=VMEM_LIMIT),
        cost_estimate=pl.CostEstimate(
            flops=20 * tokens * channels * hidden,
            bytes_accessed=12 * hidden * channels,
            transcendentals=4 * tokens * hidden,
        ),
        name="mlp",
    )(core, order, mine, theirs, gb_mine, gb_theirs, bias, second, *pieces)


def unnorm_kernel(gn_ref, gn_other_ref, std_ref, inv_ref, gain_ref, grad_conv_ref, channel_ref):
    step = pl.program_id(0)
    channels = gn_ref.shape[1]
    parts = [slice(c, c + LANES) for c in range(0, channels, LANES)]
    gain = [gain_ref[:, c] for c in parts]
    tall = 32

    @pl.when(step == 0)
    def _():
        channel_ref[...] = jnp.zeros_like(channel_ref)

    def one(i, sums):
        at = pl.ds(pl.multiple_of(i * tall, tall), tall)
        inv = inv_ref[at, :]
        scaled, new = [], []
        for c, lanes in enumerate(parts):
            gn = gn_ref[at, lanes] + gn_other_ref[at, lanes].astype(F32)
            std = std_ref[at, lanes]
            product = gn * std
            gain_sum, shift_sum = sums[2 * c], sums[2 * c + 1]
            for r in range(0, tall, SUBLANES):
                gain_sum = gain_sum + product[r : r + SUBLANES]
                shift_sum = shift_sum + gn[r : r + SUBLANES]
            new += [gain_sum, shift_sum]
            scaled.append((gn * gain[c], product * gain[c], std))
        mean = sum(jnp.sum(v[0], axis=1, keepdims=True) for v in scaled) / channels
        mean_std = sum(jnp.sum(v[1], axis=1, keepdims=True) for v in scaled) / channels
        for c, (v, _, std) in enumerate(scaled):
            grad_conv_ref[at, parts[c]] = inv * (v - mean - std * mean_std)
        return tuple(new)

    zero = jnp.zeros((SUBLANES, LANES), F32)
    sums = lax.fori_loop(0, NORM_BLOCK // tall, one, (zero,) * (2 * len(parts)))
    for c, lanes in enumerate(parts):
        channel_ref[0:1, lanes] += jnp.sum(sums[2 * c], axis=0, keepdims=True)
        channel_ref[1:2, lanes] += jnp.sum(sums[2 * c + 1], axis=0, keepdims=True)


def unnorm(gn, gn_other, std, inv, gain):
    tokens, channels = gn.shape
    block = pl.BlockSpec((NORM_BLOCK, channels), lambda j: (j, 0))
    return pl.pallas_call(
        unnorm_kernel,
        grid=(tokens // NORM_BLOCK,),
        in_specs=[
            block, block, block,
            pl.BlockSpec((NORM_BLOCK, 1), lambda j: (j, 0)),
            whole((1, channels)),
        ],
        out_specs=[block, whole((2, channels))],
        out_shape=[
            jax.ShapeDtypeStruct((tokens, channels), F32),
            jax.ShapeDtypeStruct((2, channels), F32),
        ],
        compiler_params=pltpu.CompilerParams(vmem_limit_bytes=SMALL_VMEM),
        cost_estimate=pl.CostEstimate(
            flops=20 * tokens * channels, bytes_accessed=14 * tokens * channels, transcendentals=0
        ),
        name="unnorm",
    )(gn, gn_other, std, inv, gain)


def load_grads(grad_ref, rows, grad_minor, groups, tokens):
    rows[:tokens, :] = grad_ref[...]
    if rows.shape[0] > tokens:
        rows[tokens:, :] = jnp.zeros((rows.shape[0] - tokens, LANES), F32)
    to_patch_minor(rows, grad_minor, groups)


def taps_kernel(
    slots, x_ref, grad_ref, _after, _buffer, grad_taps_ref, rows, minor, grad_minor, tap_sums
):
    groups = rows.shape[0] // (SUBLANES * SPOTS)
    load_grads(grad_ref, rows, grad_minor, groups, slots * SPOTS)

    def load(slot, _):
        rows[pl.ds(pl.multiple_of(slot * SPOTS, SPOTS), SPOTS), :] = (
            x_ref[slot].astype(F32).reshape(SPOTS, LANES)
        )
        return 0

    lax.fori_loop(0, slots, load, 0)
    to_patch_minor(rows, minor, groups)

    def taps(group, _):
        for a in range(TAPS):
            sums = [jnp.where(group == 0, 0.0, tap_sums[a * TAPS + b]) for b in range(TAPS)]
            for p in range(SIDE):
                row = p + a - REACH
                if not 0 <= row < SIDE:
                    continue
                values = [minor[group * SPOTS + row * SIDE + q] for q in range(SIDE)]
                grads = [grad_minor[group * SPOTS + p * SIDE + q] for q in range(SIDE)]
                for b in range(TAPS):
                    for q in range(SIDE):
                        col = q + b - REACH
                        if 0 <= col < SIDE:
                            sums[b] = sums[b] + grads[q] * values[col]
            for b in range(TAPS):
                tap_sums[a * TAPS + b] = sums[b]
        return 0

    lax.fori_loop(0, groups, taps, 0)
    for tap in range(TAPS * TAPS):
        grad_taps_ref[tap : tap + 1, :] = jnp.sum(tap_sums[tap], axis=0, keepdims=True)


def taps_part(part, x, grad_conv, after, buffer):
    slots, channels, tokens, groups, padded = shapes_of(x)
    base = part * GROUP_STEPS
    anywhere = pl.BlockSpec(memory_space=pl.ANY)
    if buffer is None:
        buffer, aliases = after, {}
    else:
        aliases = {3: 0}
    return pl.pallas_call(
        functools.partial(taps_kernel, slots),
        grid=(GROUP_STEPS,),
        in_specs=[
            pl.BlockSpec((slots, SIDE, SIDE, LANES), lambda j: (0, 0, 0, j + base)),
            pl.BlockSpec((tokens, LANES), lambda j: (0, j + base)),
            anywhere,
            anywhere,
        ],
        out_specs=pl.BlockSpec((TAPS * TAPS, LANES), lambda j: (0, j + base)),
        out_shape=jax.ShapeDtypeStruct((TAPS * TAPS, channels), F32),
        input_output_aliases=aliases,
        scratch_shapes=[
            pltpu.VMEM((padded, LANES), F32),
            pltpu.VMEM((groups * SPOTS, SUBLANES, LANES), F32),
            pltpu.VMEM((groups * SPOTS, SUBLANES, LANES), F32),
            pltpu.VMEM((TAPS * TAPS, SUBLANES, LANES), F32),
        ],
        compiler_params=pltpu.CompilerParams(vmem_limit_bytes=SMALL_VMEM),
        cost_estimate=pl.CostEstimate(
            flops=2 * 49 * tokens * LANES * GROUP_STEPS,
            bytes_accessed=6 * tokens * LANES * GROUP_STEPS,
            transcendentals=0,
        ),
        name="taps",
    )(x, grad_conv, after, buffer)


def back_kernel(
    slots, g_ref, grad_ref, count_ref, taps_ref, _after, _buffer, in_grad_ref,
    rows, grad_minor, spread, result,
):
    groups = rows.shape[0] // (SUBLANES * SPOTS)
    spread_taps(taps_ref, spread)
    load_grads(grad_ref, rows, grad_minor, groups, slots * SPOTS)

    def convolve(group, _):
        def emit(spot, value):
            result[pl.ds(group * SUBLANES * SPOTS + spot, SUBLANES, stride=SPOTS), :] = value

        conv_rows(grad_minor, spread, group, True, emit)
        return 0

    lax.fori_loop(0, groups, convolve, 0)
    count = count_ref[0, 0]

    def finish(slot, _):
        live = jnp.where(slot < count, 1.0, 0.0)
        g = g_ref[slot].astype(F32) * live
        at = pl.ds(pl.multiple_of(slot * SPOTS, SPOTS), SPOTS)
        in_grad_ref[slot] = g + result[at, :].reshape(SIDE, SIDE, LANES)
        return 0

    lax.fori_loop(0, slots, finish, 0)


def back_part(part, g, grad_conv, count, taps, after, buffer):
    slots, channels, tokens, groups, padded = shapes_of(g)
    base = part * GROUP_STEPS
    anywhere = pl.BlockSpec(memory_space=pl.ANY)
    if buffer is None:
        buffer, aliases = after, {}
    else:
        aliases = {5: 0}
    return pl.pallas_call(
        functools.partial(back_kernel, slots),
        grid=(GROUP_STEPS,),
        in_specs=[
            pl.BlockSpec((slots, SIDE, SIDE, LANES), lambda j: (0, 0, 0, j + base)),
            pl.BlockSpec((tokens, LANES), lambda j: (0, j + base)),
            pl.BlockSpec(memory_space=pltpu.SMEM),
            pl.BlockSpec((TAPS * TAPS, LANES), lambda j: (0, j + base)),
            anywhere,
            anywhere,
        ],
        out_specs=pl.BlockSpec((slots, SIDE, SIDE, LANES), lambda j: (0, 0, 0, j + base)),
        out_shape=jax.ShapeDtypeStruct((slots, SIDE, SIDE, channels), F32),
        input_output_aliases=aliases,
        scratch_shapes=[
            pltpu.VMEM((padded, LANES), F32),
            pltpu.VMEM((groups * SPOTS, SUBLANES, LANES), F32),
            pltpu.VMEM((TAPS * TAPS, SUBLANES, LANES), F32),
            pltpu.VMEM((padded, LANES), F32),
        ],
        compiler_params=pltpu.CompilerParams(vmem_limit_bytes=SMALL_VMEM),
        cost_estimate=pl.CostEstimate(
            flops=2 * 49 * tokens * LANES * GROUP_STEPS,
            bytes_accessed=10 * tokens * LANES * GROUP_STEPS,
            transcendentals=0,
        ),
        name="back",
    )(g, grad_conv, count, taps, after, buffer)


def device_index(x, y, z, core):
    high, low = divmod(y % Y, 2)
    return ((x % X) * 4 + high * 2 + core) * (2 * Z) + (z % Z) * 2 + low


def move(value, dy=0, dz=0, flip=0):
    pairs = [
        (device_index(x, y, z, core), device_index(x, y + dy, z + dz, core ^ flip))
        for x in range(X)
        for y in range(Y)
        for z in range(Z)
        for core in range(2)
    ]
    return lax.ppermute(value, AXES, pairs)


def gather_pieces(piece, z, low, between):
    other = lax.ppermute(piece, "fsdp", [(i, i ^ 1) for i in range(2 * Z)])
    pair = jnp.concatenate([piece, other])
    right, left = move(pair, dz=1), move(pair, dz=-1)
    right, left, made = between(right, left)
    pieces, away = [pair, right, left], [0, Z - 1, 1]
    for step in range(2, Z // 2 + 1):
        right = move(right, dz=1)
        pieces.append(right)
        away.append(Z - step)
        if step < Z // 2:
            left = move(left, dz=-1)
            pieces.append(left)
            away.append(step)
    order = [(z + s) % Z * 2 + (low ^ parity) for s in away for parity in range(2)]
    return jnp.stack(order).astype(jnp.int32), pieces, made


def copies_kernel(kept_ref, swapped_ref, _right, _left, out_ref, _right_out, _left_out):
    def shard(f, _):
        both = [kept_ref[f].astype(F32), swapped_ref[f].astype(F32)]
        both = jnp.concatenate(both).astype(BF16)
        rows = both.shape[0]
        for e in range(out_ref.shape[0]):
            out_ref[e, pl.ds(pl.multiple_of(f * rows, rows), rows), :] = both
        return 0

    lax.fori_loop(0, kept_ref.shape[0], shard, 0)


def copies(chips, kept, swapped, right, left):
    shards, rows, lanes = kept.shape
    vmem = pl.BlockSpec(memory_space=pltpu.VMEM)
    anywhere = pl.BlockSpec(memory_space=pl.ANY)
    return pl.pallas_call(
        copies_kernel,
        in_specs=[vmem, vmem, anywhere, anywhere],
        out_specs=[vmem, anywhere, anywhere],
        out_shape=[
            jax.ShapeDtypeStruct((chips, shards * 2 * rows, lanes), BF16),
            jax.ShapeDtypeStruct(right.shape, BF16),
            jax.ShapeDtypeStruct(left.shape, BF16),
        ],
        input_output_aliases={2: 1, 3: 2},
        compiler_params=pltpu.CompilerParams(vmem_limit_bytes=SMALL_VMEM),
        name="copies",
    )(kept, swapped, right, left)


def add_up_kernel(terms_ref, _after, out_ref):
    tall = 8 * SUBLANES

    def rows(i, _):
        at = pl.ds(pl.multiple_of(i * tall, tall), tall)
        total = terms_ref[0, at, :].astype(F32)
        for e in range(1, terms_ref.shape[0]):
            total = total + terms_ref[e, at, :].astype(F32)
        out_ref[at, :] = total.astype(BF16)
        return 0

    lax.fori_loop(0, terms_ref.shape[1] // tall, rows, 0, unroll=2)


def add_up(terms, after):
    return pl.pallas_call(
        add_up_kernel,
        in_specs=[
            pl.BlockSpec(memory_space=pltpu.VMEM),
            pl.BlockSpec(memory_space=pl.ANY),
        ],
        out_shape=jax.ShapeDtypeStruct(terms.shape[1:], BF16),
        compiler_params=pltpu.CompilerParams(vmem_limit_bytes=SMALL_VMEM),
        name="add_up",
    )(terms, after)


def finish_kernel(
    factor, place_ref, mine_ref, theirs_ref, first_ref, second_ref, small_ref
):
    core, side = place_ref[0], place_ref[1]
    small_rows = PART_TILES * 2 * SUBLANES
    half = small_rows // 2
    wide = first_ref.shape[1] // 2 // LANES
    small = None
    for e in range(mine_ref.shape[0]):
        mine, theirs = mine_ref[e].astype(F32), theirs_ref[e].astype(F32)
        for k in range(2):
            part = jnp.where(core == k, mine[:half], theirs[:half]) * factor
            for i in range(PART_TILES):
                r, c = tile_of(e, i, wide)
                if r * SUBLANES < first_ref.shape[0]:
                    lane = (k * wide + c) * LANES
                    first_ref[r * SUBLANES : (r + 1) * SUBLANES, lane : lane + LANES] = part[
                        i * SUBLANES : (i + 1) * SUBLANES
                    ]
        more = mine[small_rows:] + theirs[small_rows:]
        small = more if small is None else small + more
        mine, theirs = mine[half:small_rows], theirs[half:small_rows]
        part = jnp.concatenate(
            [jnp.where(core == side, mine, theirs), jnp.where(core == side, theirs, mine)]
        )
        part = part * factor
        for i in range(PART_TILES):
            r, c = tile_of(e, i, second_ref.shape[1] // LANES)
            if r * 2 * SUBLANES < second_ref.shape[0]:
                second_ref[r * 2 * SUBLANES : (r + 1) * 2 * SUBLANES, c * LANES : (c + 1) * LANES] = (
                    part[i * 2 * SUBLANES : (i + 1) * 2 * SUBLANES]
                )
    small_ref[...] = small * factor


def finish(place, mine, theirs, first_shape, second_shape, factor):
    small = (mine.shape[1] - PART_TILES * 2 * SUBLANES, LANES)
    vmem = pl.BlockSpec(memory_space=pltpu.VMEM)
    return pl.pallas_call(
        functools.partial(finish_kernel, factor),
        in_specs=[pl.BlockSpec(memory_space=pltpu.SMEM), vmem, vmem],
        out_shape=[
            jax.ShapeDtypeStruct(first_shape, F32),
            jax.ShapeDtypeStruct(second_shape, F32),
            jax.ShapeDtypeStruct(small, F32),
        ],
        compiler_params=pltpu.CompilerParams(vmem_limit_bytes=SMALL_VMEM),
        name="finish",
    )(place, mine, theirs)


def pack(rows):
    count, width = rows.shape[-2:]
    half = -(-count // 2)
    lead = [(0, 0)] * (rows.ndim - 2)
    rows = jnp.pad(rows, lead + [(0, 2 * half - count), (0, 0)])
    rows = jnp.concatenate([rows[..., :half, :], rows[..., half:, :]], axis=-1)
    return jnp.pad(rows, lead + [(0, -half % (2 * SUBLANES)), (0, LANES - 2 * width)])


def unpack(packed, count, width):
    half = -(-count // 2)
    rows = [packed[..., :half, :width], packed[..., :half, width : 2 * width]]
    return jnp.concatenate(rows, axis=-2)[..., :count, :]


def local(
    patches,
    out_grad,
    row_counts,
    dw_kernel,
    ln_gain,
    ln_bias,
    w_first,
    first_bias,
    w_second,
    layer_scale,
):
    fsdp, dp = lax.axis_size("fsdp"), lax.axis_size("dp")
    own = ln_gain.shape[0]
    units = first_bias.shape[0]
    channels, hidden = own * fsdp, units * fsdp
    mine = hidden // 2
    tap_count = dw_kernel.shape[0]
    dp_index, fsdp_index = lax.axis_index("dp"), lax.axis_index("fsdp")
    core = dp_index % 2
    z, low = fsdp_index // 2, fsdp_index % 2

    chip, chips = dp_index // 2, dp // 2
    side = fsdp_index // (fsdp // 2)
    same_core = [[2 * i + c for i in range(chips)] for c in range(2)]
    flat = (PART_TILES * SUBLANES, LANES)

    tall, across = units // (2 * SUBLANES), channels // LANES
    tiles = w_second.reshape(tall, 2 * SUBLANES, across, LANES).transpose(0, 2, 1, 3)
    tiles = tiles.reshape(tall * across, 2 * SUBLANES, LANES)
    tiles = jnp.pad(tiles, ((0, chips * PART_TILES - tall * across), (0, 0), (0, 0)))
    tiles = tiles.reshape(chips * 2, *flat)
    tiles = lax.dynamic_index_in_dim(tiles, 2 * chip + (core ^ side), 0, keepdims=False)
    vectors = [ln_gain[None], ln_bias[None], layer_scale[None], first_bias.reshape(-1, own)]
    small = jnp.concatenate([dw_kernel] + vectors)
    lines = small.shape[0]
    small = jnp.concatenate([tiles, pack(small)])
    small = lax.all_to_all(
        jnp.broadcast_to(small, (fsdp,) + small.shape), "fsdp", 0, 0, tiled=True
    )
    tiles, small = small[:, : flat[0]], unpack(small[:, flat[0] :], lines, own)
    kept = lax.dynamic_slice_in_dim(tiles, core * (fsdp // 2), fsdp // 2)
    swapped = move(lax.dynamic_slice_in_dim(tiles, (1 - core) * (fsdp // 2), fsdp // 2), flip=1)

    def between(right, left):
        made, right, left = copies(chips, kept, swapped, right, left)
        made = lax.all_to_all(made, "dp", 0, 0, tiled=True, axis_index_groups=same_core)
        return right, left, made

    part = lax.dynamic_slice_in_dim(w_first, core * mine, mine, 1)
    part = [part[:, k * CUT : (k + 1) * CUT] for k in range(mine // CUT)]
    order, pieces, second = gather_pieces(jnp.concatenate(part), z, low, between)

    taps = small[:, :tap_count].transpose(1, 0, 2).reshape(tap_count, channels).astype(F32)
    gain, shift, scale = (
        small[:, tap_count + i].reshape(1, channels).astype(F32) for i in range(3)
    )
    bias = small[:, tap_count + 3 :].reshape(1, hidden).astype(F32)
    bias = lax.dynamic_slice_in_dim(bias, core * mine, mine, 1)

    x, g = patches[0], out_grad[0]
    conv = conv_part(0, x, taps, pieces[1], None)
    conv = conv_part(1, x, taps, pieces[4], conv)
    conv = conv_part(2, x, taps, pieces[6], conv)
    normed, std, inv, gb = norm(conv, g, row_counts, gain, shift, scale, pieces[7])
    normed_other, gb_other = move(normed, flip=1), move(gb, flip=1)
    terms, gn_mine, gn_theirs, grad_bias, scale_sum = mlp(
        core.reshape(1), order, normed, normed_other, gb, gb_other, bias, second, pieces
    )
    gn_other = move(gn_theirs, flip=1)
    scale_sum = scale_sum / scale
    grad_conv, channel_sums = unnorm(gn_mine, gn_other, std, inv, gain)
    grad_taps = taps_part(0, x, grad_conv, terms, None)
    grad_taps = taps_part(1, x, grad_conv, terms, grad_taps)
    grad_taps = taps_part(2, x, grad_conv, terms, grad_taps)
    in_grad = back_part(0, g, grad_conv, row_counts, taps, terms, None)
    in_grad = back_part(1, g, grad_conv, row_counts, taps, terms, in_grad)
    in_grad = back_part(2, g, grad_conv, row_counts, taps, terms, in_grad)

    terms = lax.all_to_all(terms, "dp", 0, 0, tiled=True, axis_index_groups=same_core)
    terms = add_up(terms, in_grad)
    first = terms[: fsdp * flat[0]].reshape((fsdp,) + flat)
    second = terms[fsdp * flat[0] :].reshape((fsdp // 2, 2) + flat)
    swapped = move(second[:, 1], flip=1)
    second = jnp.where(
        core == 0,
        jnp.concatenate([second[:, 0], swapped]),
        jnp.concatenate([swapped, second[:, 0]]),
    )
    sums = jnp.concatenate([grad_taps, channel_sums, scale_sum], axis=0)
    sums = sums.reshape(sums.shape[0], fsdp, own).transpose(1, 0, 2)
    grad_bias = jnp.concatenate([grad_bias, grad_bias], axis=1).reshape(fsdp, -1, own)
    computed = (jnp.arange(fsdp, dtype=jnp.int32) // (fsdp // 2) == core)[:, None, None]
    sums = jnp.concatenate([sums, jnp.where(computed, grad_bias, 0.0)], axis=1)
    terms = jnp.concatenate([first, second, pack(sums.astype(BF16))], axis=1)
    terms = lax.all_to_all(terms, "fsdp", 0, 0, tiled=True)
    terms = jnp.sum(terms.astype(F32), axis=0).astype(BF16)
    terms = lax.all_to_all(
        jnp.broadcast_to(terms[None], (chips,) + terms.shape),
        "dp", 0, 0, tiled=True, axis_index_groups=same_core,
    )
    factor = 1.0 / math.sqrt(fsdp * dp * ROWS * SPOTS)
    first, second, sums = finish(
        jnp.stack([core, side]).astype(jnp.int32),
        terms,
        move(terms, flip=1),
        (own, hidden),
        (units, channels),
        factor,
    )
    sums = unpack(sums, lines, own)
    return (
        in_grad[None],
        first,
        second,
        sums[:tap_count],
        sums[tap_count + 3 :].reshape(units),
        sums[tap_count : tap_count + 3],
    )


def solution(mesh):
    placed = (
        P("fsdp", "dp", None, None, None),
        P("fsdp", "dp", None, None, None),
        P("fsdp", "dp"),
        P(None, "fsdp"),
        P("fsdp"),
        P("fsdp"),
        P("fsdp", None),
        P("fsdp"),
        P("fsdp", None),
        P("fsdp"),
    )
    return jax.shard_map(
        local,
        mesh=mesh,
        in_specs=placed,
        out_specs=(
            P("fsdp", "dp", None, None, None),
            P("fsdp", None),
            P("fsdp", None),
            P(None, "fsdp"),
            P("fsdp"),
            P(None, "fsdp"),
        ),
        check_vma=False,
    )
```
